32 devices in a mesh: wide: 8 (over y, x, core), narrow: 4 (over z).
Axes of the slice: x: 2, y: 2, z: 4, core: 2. Of those that a mesh axis runs over, the one named last changes fastest.
Arguments:
- tokens: bfloat16 [4096, 2048], P(('wide', 'narrow')), may hold values from -6 to 6
- out_grad: bfloat16 [4096, 2048], P(('wide', 'narrow')), may hold values from -6 to 6
- routes: int32 [4096, 4], P(('wide', 'narrow')), may hold values from 0 to 31, all different within a row; in each aligned block of 128 rows (0 to 127, 128 to 255, ...) at most 32 rows name the same one
- route_gates: float32 [4096, 4], P(('wide', 'narrow')), may hold values from 0.05 to 0.4
- expert_weights: bfloat16 [2048, 32, 2304], P('narrow', 'wide'), may hold values from -0.21875 to 0.21875
Outputs:
- layer_output: bfloat16 [4096, 2048], P(('wide', 'narrow'))
- token_grad: bfloat16 [4096, 2048], P(('wide', 'narrow'))
- gate_grad: float32 [4096, 4], P(('wide', 'narrow'))
- weight_grad: bfloat16 [2048, 32, 2304], P('narrow', 'wide')
The draws below stay inside these ranges and needn't reach their ends.
Inputs may be any that keep to these rules, and one draw needn't show every extreme that they name: `routes`: each row names 4 different experts. Among the 128 tokens of one device no expert is named by more than 32 of them, and in every draw some device's tokens name some expert exactly 32 times.
All inputs are finite; a program needn't handle non-finite values.
Results may differ from the reference program's by a relative error of at most 0.0064.
Values may be sent and summed in bfloat16 or wider, within the bound.
No kernel may reach another device: no remote copies, remote signals or barrier semaphores. Data moves between devices by JAX's collectives and lax.ppermute only.
A program may use at most 192 MiB of HBM per device.

```python
import math
import jax
import jax.numpy as jnp
import numpy as np
from jax import lax

D = 2048
H = 768
TOP = 4
TOK_DEV = 128
EXPERTS = 32
CAP = 32
TOKENS = 4096
N_WIDE = 8
N_NARROW = 4


def shard_levels(stream_key, extent, pieces, least, high):
    gain = 1.0
    for dim, shards_of in pieces:
        heights = jax.random.uniform(jax.random.fold_in(jax.random.fold_in(stream_key, 6), dim), (shards_of,), jnp.float32, least / len(pieces), high / len(pieces))
        gain = gain * jnp.repeat(jnp.exp(heights), extent[dim] // shards_of).reshape((-1,) + (1,) * (len(extent) - 1 - dim))
    return gain


def routed_block(stream_key, own, number, rows, amount, top, reach, lean):
    ranking = jax.random.permutation(stream_key, amount)
    packed, common = load_shares(amount, rows * top, reach, lean, True), load_shares(amount, rows * top, reach, lean, False)
    places = jnp.arange(amount)

    def named(lengths, rotation):
        used = int((lengths > 0).sum())
        fixed = max(1, used // 4)
        passed = fixed + (places - fixed + rotation * (used - fixed)) % max(1, amount - fixed)
        return jnp.zeros((amount,), jnp.int32).at[ranking[jnp.where(places < fixed, places, passed)]].set(jnp.asarray(lengths, jnp.int32))

    lengths = jnp.where(number % 4 == 0, named(packed, number // 4), named(common, number - number // 4 - 1))
    mixed = jax.random.permutation(jax.random.fold_in(own, 3), amount)
    giver, receiver = mixed[0:amount // 2 * 2:2], mixed[1:amount // 2 * 2:2]
    room = jnp.minimum(lengths[giver] - 1, reach - lengths[receiver]) // 2
    room = jnp.where((giver == ranking[0]) | (receiver == ranking[0]) | (lengths[receiver] == 0), 0, jnp.maximum(room, 0))
    passed = jax.random.randint(jax.random.fold_in(own, 4), (amount // 2,), 0, 1 << 20) % (room + 1)
    lengths = lengths.at[giver].add(-passed).at[receiver].add(passed)
    items = jnp.searchsorted(jnp.cumsum(lengths), jnp.arange(rows * top), side="right").astype(jnp.int32)
    listing = items.reshape(top, rows).T
    listing = listing[jax.random.permutation(jax.random.fold_in(own, 1), rows)]
    rotation = jax.random.randint(jax.random.fold_in(own, 2), (rows, 1), 0, top)
    return jnp.take_along_axis(listing, (jnp.arange(top)[None, :] + rotation) % top, axis=1)


def load_shares(number_of, total, limit, slope, full):
    portions = [(1 << 20) // math.isqrt(grade ** slope) + 1 for grade in range(1, number_of + 1)]
    largest = limit if full else min(limit, max(-(-total // number_of), total * portions[0] // sum(portions)))
    least = 1 if total - largest >= number_of - 1 else 0
    counts, rest = [largest] + [least] * (number_of - 1), total - largest - least * (number_of - 1)
    while rest > 0:
        free = [i for i in range(1, number_of) if counts[i] < largest] or [i for i in range(1, number_of) if counts[i] < limit]
        whole, left = sum([portions[i] for i in free]), rest
        for i in free:
            more = min(limit - counts[i], max(1, left * portions[i] // whole), rest)
            counts[i] = counts[i] + more
            rest = rest - more
    return np.array(counts)


def noise(key, shape, spread, limit, split=(), kind=jnp.bfloat16):
    array = jax.random.normal(key, shape, jnp.float32) * spread
    if len(split) > 0:
        array = shard_levels(key, shape, split, -0.22, 0.18) * array
    return jnp.clip(array, min=-limit, max=limit).astype(kind)


def setup_inputs(seed: int = 0) -> dict:
    keys = jax.random.split(jax.random.key(seed), 6)
    tokens = noise(keys[0], (TOKENS, D), 1.0, 6.0, ((0, 32),))
    out_grad = noise(keys[1], (TOKENS, D), 1.0, 6.0, ((0, 32),))
    routes_keys = jax.random.split(jax.random.fold_in(keys[2], 1), TOKENS // TOK_DEV)
    routes_turns = jax.random.permutation(jax.random.fold_in(keys[2], 3), TOKENS // TOK_DEV)
    routes = jax.vmap(lambda own, number: routed_block(jax.random.fold_in(keys[2], 2), own, number, TOK_DEV, EXPERTS, TOP, CAP, 2))(routes_keys, routes_turns).reshape((TOKENS, TOP))
    route_gates = jnp.clip(0.05 + 0.35 * jax.random.uniform(keys[3], (TOKENS, TOP), jnp.float32) ** shard_levels(keys[3], (TOKENS, TOP), ((0, 32),), -0.2, 0.2), 0.05, 0.4)
    expert_weights = noise(keys[4], (D, EXPERTS, 3 * H), H ** -0.5, 0.21875, ((0, 4), (1, 8)))
    return {"tokens": tokens, "out_grad": out_grad, "routes": routes, "route_gates": route_gates, "expert_weights": expert_weights}


def expert_pass(weights, rows_in, cotangent):
    hidden_units = weights.shape[1] // 3
    w_gate = weights[:, :hidden_units]
    w_up = weights[:, hidden_units:2 * hidden_units]
    w_down = weights[:, 2 * hidden_units:]
    gate_pre = jnp.dot(rows_in, w_gate, preferred_element_type=jnp.float32)
    up_pre = jnp.dot(rows_in, w_up, preferred_element_type=jnp.float32)
    sigmoid = jax.nn.sigmoid(gate_pre)
    activated = gate_pre * sigmoid
    hidden = (activated * up_pre).astype(jnp.bfloat16)
    expert_out = jnp.dot(hidden, w_down.T, preferred_element_type=jnp.float32).astype(jnp.bfloat16)
    hidden_grad = jnp.dot(cotangent, w_down, preferred_element_type=jnp.float32)
    slope_term = sigmoid * (1.0 + gate_pre * (1.0 - sigmoid))
    gate_part = (hidden_grad * up_pre * slope_term).astype(jnp.bfloat16)
    up_part = (hidden_grad * activated).astype(jnp.bfloat16)
    both_part = jnp.concatenate([gate_part, up_part], axis=1)
    row_grad = jnp.dot(both_part, weights[:, :2 * hidden_units].T, preferred_element_type=jnp.float32).astype(jnp.bfloat16)
    weight_in_grad = jnp.dot(rows_in.T, both_part, preferred_element_type=jnp.float32)
    weight_down_grad = jnp.dot(cotangent.T, hidden, preferred_element_type=jnp.float32)
    return expert_out, row_grad, jnp.concatenate([weight_in_grad, weight_down_grad], axis=1)


def reference(tokens, out_grad, routes, route_gates, expert_weights):
    devices = N_WIDE * N_NARROW
    copies = TOK_DEV * TOP
    flat_routes = routes.reshape(devices, copies)
    onehot = (flat_routes[:, :, None] == jnp.arange(EXPERTS, dtype=jnp.int32)[None, None, :]).astype(jnp.int32)
    copy_rank = jnp.sum(jnp.cumsum(onehot, axis=1) * onehot, axis=2) - 1
    device_ids = jnp.arange(devices, dtype=jnp.int32)[:, None]
    slot_ids = (flat_routes * (devices * CAP) + device_ids * CAP + copy_rank).reshape(-1).astype(jnp.int32)
    slot_table = jnp.full((EXPERTS * devices * CAP,), -1, jnp.int32)
    slot_table = slot_table.at[slot_ids].set(jnp.arange(devices * copies, dtype=jnp.int32))
    slot_table = slot_table.reshape(EXPERTS, devices * CAP)
    flat_gates = route_gates.reshape(-1)
    weights_by_expert = jnp.transpose(expert_weights, (1, 0, 2))

    def one_expert(operands):
        weights, entries = operands
        present = entries >= 0
        safe_ids = jnp.maximum(entries, 0)
        token_ids = safe_ids // TOP
        rows_in = jnp.where(present[:, None], tokens[token_ids], jnp.zeros((), tokens.dtype))
        scaled = flat_gates[safe_ids][:, None] * out_grad[token_ids].astype(jnp.float32)
        cotangent = jnp.where(present[:, None], scaled, jnp.zeros((), jnp.float32)).astype(jnp.bfloat16)
        expert_out, row_grad, weight_grad = expert_pass(weights, rows_in, cotangent)
        return expert_out, row_grad, weight_grad.astype(jnp.bfloat16)

    expert_outs, row_grads, weight_grads = lax.map(one_expert, (weights_by_expert, slot_table))
    weight_grad = jnp.transpose(weight_grads, (1, 0, 2))
    copy_outs = expert_outs.reshape(-1, D)[slot_ids].reshape(TOKENS, TOP, D).astype(jnp.float32)
    copy_grads = row_grads.reshape(-1, D)[slot_ids].reshape(TOKENS, TOP, D).astype(jnp.float32)
    layer_output = jnp.sum(route_gates[:, :, None] * copy_outs, axis=1).astype(jnp.bfloat16)
    gate_grad = jnp.sum(out_grad.astype(jnp.float32)[:, None, :] * copy_outs, axis=2)
    token_grad = jnp.sum(copy_grads, axis=1).astype(jnp.bfloat16)
    return layer_output, token_grad, gate_grad, weight_grad
```

```python
import functools

import jax
import jax.numpy as jnp
from jax import lax
from jax.experimental import pallas as pl
from jax.experimental.pallas import tpu as pltpu
from jax.sharding import PartitionSpec as P

F32 = jnp.float32
BF16 = jnp.bfloat16
VMEM_LIMIT = 56 * 1024 * 1024


def dot(a, b, dims):
    return lax.dot_general(a, b, (dims, ((), ())), preferred_element_type=F32)


def params():
    return pltpu.CompilerParams(vmem_limit_bytes=VMEM_LIMIT)


def whole(shape):
    return pl.BlockSpec(shape, lambda *_: (0,) * len(shape))


def chain_gather(x, axis, me):
    n = lax.axis_size(axis)
    ups, downs = [], []
    up = down = x
    for step in range(1, n):
        up = lax.ppermute(up, axis, [(i, i + 1) for i in range(step - 1, n - 1)])
        down = lax.ppermute(down, axis, [(i, i - 1) for i in range(1, n - step + 1)])
        ups.append(up)
        downs.append(down)
    line = jnp.stack(ups[::-1] + [x] + downs)
    return lax.dynamic_slice_in_dim(line, n - 1 - me, n, 0)


def chain_scatter(parts, axis, me):
    n = lax.axis_size(axis)

    def part(i):
        return lax.dynamic_index_in_dim(parts, jnp.clip(i, 0, n - 1), 0, keepdims=False)

    up = down = None
    for step in range(1, n):
        far = n - step
        up_send = part(me + far)
        down_send = part(me - far)
        if up is not None:
            up_send = (up_send.astype(F32) + up.astype(F32)).astype(BF16)
            down_send = (down_send.astype(F32) + down.astype(F32)).astype(BF16)
        up = lax.ppermute(up_send, axis, [(i, i + 1) for i in range(step)])
        down = lax.ppermute(down_send, axis, [(i, i - 1) for i in range(n - step, n)])
    total = part(me).astype(F32) + up.astype(F32) + down.astype(F32)
    return total.astype(BF16)


def slot_matrix(ranks, capacity):
    groups, tokens = ranks.shape
    slot = lax.broadcasted_iota(jnp.int32, (groups, capacity, tokens), 1)
    return ranks[:, None, :] == slot


def dispatch_kernel(level_ref, ranks_ref, x_ref, out_ref):
    groups, _, capacity, width = out_ref.shape
    tokens = x_ref.shape[1]
    taken = slot_matrix(ranks_ref[0], capacity)
    matrix = jnp.where(taken, 1.0, 0.0).astype(BF16).reshape(groups * capacity, tokens)
    rows = dot(matrix, x_ref[0], ((1,), (0,)))
    out_ref[...] = rows.astype(BF16).reshape(groups, 1, capacity, width)


def gated_dispatch_kernel(level_ref, ranks_ref, gates_ref, x_ref, out_ref):
    groups, _, capacity, width = out_ref.shape
    tokens = x_ref.shape[1]
    taken = slot_matrix(ranks_ref[0], capacity)
    matrix = jnp.where(taken, 1.0, 0.0).astype(BF16).reshape(groups * capacity, tokens)
    gates = jnp.sum(jnp.where(taken, gates_ref[0][:, None, :], 0.0), axis=2, keepdims=True)
    rows = dot(matrix, x_ref[0], ((1,), (0,)))
    rows = rows * gates.reshape(groups * capacity, 1)
    out_ref[...] = rows.astype(BF16).reshape(groups, 1, capacity, width)


def dispatch(level, ranks, x, capacity, gates=None):
    sources, groups, tokens = ranks.shape
    model = x.shape[2]
    width = model // sources
    per_source = pl.BlockSpec((1, groups, tokens), lambda s, k, level: (s, 0, 0))
    x_spec = pl.BlockSpec(
        (1, tokens, width), lambda s, k, level: (s, 0, lax.rem(level[0] - k + sources, sources))
    )
    extra = [] if gates is None else [gates]
    return pl.pallas_call(
        dispatch_kernel if gates is None else gated_dispatch_kernel,
        out_shape=jax.ShapeDtypeStruct((groups, sources, capacity, model), BF16),
        grid_spec=pltpu.PrefetchScalarGridSpec(
            num_scalar_prefetch=1,
            grid=(sources, sources),
            in_specs=[per_source] * (1 + len(extra)) + [x_spec],
            out_specs=pl.BlockSpec(
                (groups, 1, capacity, width), lambda s, k, level: (0, s, 0, k)
            ),
        ),
        compiler_params=params(),
    )(level, ranks, *extra, x)


def combine_out_kernel(level_ref, ranks_ref, gates_ref, grad_ref, back_ref, out_ref, dots_ref):
    groups, _, capacity, width = back_ref.shape
    tokens = out_ref.shape[1]
    taken = slot_matrix(ranks_ref[0], capacity)
    weight = jnp.where(taken, gates_ref[0][:, None, :], 0.0).reshape(groups * capacity, tokens)
    high = weight.astype(BF16)
    low = (weight - high.astype(F32)).astype(BF16)
    rows = back_ref[...].reshape(groups * capacity, width)
    total = dot(high, rows, ((0,), (0,))) + dot(low, rows, ((0,), (0,)))
    out_ref[0] = total.astype(BF16)
    pairs = dot(rows, grad_ref[0], ((1,), (1,))).reshape(groups, capacity, tokens)
    part = jnp.sum(jnp.where(taken, pairs, 0.0), axis=1)

    @pl.when(pl.program_id(1) == 0)
    def _():
        dots_ref[0] = part

    @pl.when(pl.program_id(1) > 0)
    def _():
        dots_ref[0] += part


def combine_grad_kernel(level_ref, ranks_ref, back_ref, out_ref):
    groups, _, capacity, width = back_ref.shape
    tokens = out_ref.shape[1]
    taken = slot_matrix(ranks_ref[0], capacity)
    matrix = jnp.where(taken, 1.0, 0.0).astype(BF16).reshape(groups * capacity, tokens)
    rows = back_ref[...].reshape(groups * capacity, width)
    out_ref[0] = dot(matrix, rows, ((0,), (0,))).astype(BF16)


def combine(level, ranks, back, gates=None, grads=None):
    sources, groups, tokens = ranks.shape
    capacity, model = back.shape[2:]
    width = model // sources
    per_source = pl.BlockSpec((1, groups, tokens), lambda s, k, level: (s, 0, 0))
    x_spec = pl.BlockSpec(
        (1, tokens, width), lambda s, k, level: (s, 0, lax.rem(level[0] - k + sources, sources))
    )
    back_spec = pl.BlockSpec((groups, 1, capacity, width), lambda s, k, level: (0, s, 0, k))
    out_shape = jax.ShapeDtypeStruct((sources, tokens, model), BF16)
    if gates is None:
        return pl.pallas_call(
            combine_grad_kernel,
            out_shape=out_shape,
            grid_spec=pltpu.PrefetchScalarGridSpec(
                num_scalar_prefetch=1,
                grid=(sources, sources),
                in_specs=[per_source, back_spec],
                out_specs=x_spec,
            ),
            compiler_params=params(),
        )(level, ranks, back)
    return pl.pallas_call(
        combine_out_kernel,
        out_shape=(out_shape, jax.ShapeDtypeStruct((sources, groups, tokens), F32)),
        grid_spec=pltpu.PrefetchScalarGridSpec(
            num_scalar_prefetch=1,
            grid=(sources, sources),
            in_specs=[per_source, per_source, x_spec, back_spec],
            out_specs=(x_spec, per_source),
        ),
        compiler_params=params(),
    )(level, ranks, gates, grads, back)


def hidden_kernel(count, *refs):
    rows_ref, weights, (hidden_ref, active_ref, slope_ref) = (
        refs[0],
        refs[1 : 1 + count],
        refs[1 + count :],
    )
    width = weights[0].shape[0]
    units = hidden_ref.shape[1]
    pre = sum(
        dot(rows_ref[:, k * width : (k + 1) * width], weights[k][...], ((1,), (0,)))
        for k in range(count)
    )
    gate, up = pre[:, :units], pre[:, units:]
    sigmoid = jax.nn.sigmoid(gate)
    active = gate * sigmoid
    hidden_ref[...] = (active * up).astype(BF16)
    active_ref[...] = active
    slope_ref[...] = up * (sigmoid * (1.0 + gate * (1.0 - sigmoid)))


def hidden_pass(rows, weights, tile):
    slots, model = rows.shape
    units = weights[0].shape[1] // 2
    count = len(weights)
    out_spec = pl.BlockSpec((tile, units), lambda i: (i, 0))
    return pl.pallas_call(
        functools.partial(hidden_kernel, count),
        out_shape=(
            jax.ShapeDtypeStruct((slots, units), BF16),
            jax.ShapeDtypeStruct((slots, units), F32),
            jax.ShapeDtypeStruct((slots, units), F32),
        ),
        grid=(slots // tile,),
        in_specs=[pl.BlockSpec((tile, model), lambda i: (i, 0))]
        + [whole(w.shape) for w in weights],
        out_specs=(out_spec, out_spec, out_spec),
        compiler_params=params(),
    )(rows, *weights)


def down_kernel(count, *refs):
    hidden_ref, cotangent_ref, active_ref, slope_ref = refs[:4]
    weights = refs[4 : 4 + count]
    out_ref, both_ref = refs[4 + count :]
    width = weights[0].shape[0]
    hidden = hidden_ref[...]
    units = hidden.shape[1]
    grad = None
    for k in range(count):
        weight = weights[k][...]
        out_ref[:, k * width : (k + 1) * width] = dot(hidden, weight, ((1,), (1,))).astype(BF16)
        part = dot(cotangent_ref[:, k * width : (k + 1) * width], weight, ((1,), (0,)))
        grad = part if grad is None else grad + part
    both_ref[:, :units] = (grad * slope_ref[...]).astype(BF16)
    both_ref[:, units:] = (grad * active_ref[...]).astype(BF16)


def down_pass(hidden, cotangent, active, slope, weights, tile):
    slots, model = cotangent.shape
    units = hidden.shape[1]
    count = len(weights)
    unit_spec = pl.BlockSpec((tile, units), lambda i: (i, 0))
    model_spec = pl.BlockSpec((tile, model), lambda i: (i, 0))
    return pl.pallas_call(
        functools.partial(down_kernel, count),
        out_shape=(
            jax.ShapeDtypeStruct((slots, model), BF16),
            jax.ShapeDtypeStruct((slots, 2 * units), BF16),
        ),
        grid=(slots // tile,),
        in_specs=[unit_spec, model_spec, unit_spec, unit_spec]
        + [whole(w.shape) for w in weights],
        out_specs=(model_spec, pl.BlockSpec((tile, 2 * units), lambda i: (i, 0))),
        compiler_params=params(),
    )(hidden, cotangent, active, slope, *weights)


def row_grad_kernel(count, *refs):
    both_ref, weights, out_ref = refs[0], refs[1 : 1 + count], refs[1 + count]
    width = weights[0].shape[0]
    for k in range(count):
        out_ref[:, k * width : (k + 1) * width] = dot(
            both_ref[...], weights[k][...], ((1,), (1,))
        ).astype(BF16)


def row_grad_pass(both, weights, tile):
    slots, units = both.shape
    count = len(weights)
    model = count * weights[0].shape[0]
    return pl.pallas_call(
        functools.partial(row_grad_kernel, count),
        out_shape=jax.ShapeDtypeStruct((slots, model), BF16),
        grid=(slots // tile,),
        in_specs=[pl.BlockSpec((tile, units), lambda i: (i, 0))]
        + [whole(w.shape) for w in weights],
        out_specs=pl.BlockSpec((tile, model), lambda i: (i, 0)),
        compiler_params=params(),
    )(both, *weights)


def on_device(tokens, out_grad, routes, route_gates, expert_weights):
    wide_count = lax.axis_size("wide")
    levels = lax.axis_size("narrow")
    me = lax.axis_index("narrow")
    experts = wide_count * levels
    token_count, model = tokens.shape
    chosen = routes.shape[1]
    capacity = 2 * chosen * token_count // experts
    slots = experts * capacity
    width = model // levels
    units = expert_weights.shape[2] // 3
    level = me.astype(jnp.int32).reshape(1)
    tile = min(256, slots)

    all_routes = lax.all_gather(routes, "narrow")
    all_gates = lax.all_gather(route_gates, "narrow")
    all_tokens = chain_gather(tokens, "narrow", me)
    all_grads = chain_gather(out_grad, "narrow", me)

    by_expert = jnp.transpose(expert_weights, (1, 0, 2))

    def send_block(k):
        return lax.dynamic_index_in_dim(
            by_expert, lax.rem(me + k, levels), 0, keepdims=False
        )

    def shift(x, k):
        if k % levels == 0:
            return x
        return lax.ppermute(x, "narrow", [(i, (i + k) % levels) for i in range(levels)])

    w_in = [shift(send_block(k)[:, : 2 * units], k) for k in range(levels)]
    w_down = [shift(send_block(k)[:, 2 * units :], k) for k in range(levels)]

    mine = jnp.arange(wide_count, dtype=jnp.int32) * levels + me
    named = all_routes[:, None, :, :] == mine[None, :, None, None]
    named_any = jnp.any(named, axis=3)
    count = jnp.cumsum(named_any.astype(jnp.int32), axis=2)
    ranks = jnp.where(named_any, count - 1, -1)
    gates = jnp.sum(jnp.where(named, all_gates[:, None, :, :], 0.0), axis=3)

    def swap(x):
        return lax.all_to_all(x, "wide", split_axis=0, concat_axis=0, tiled=True)

    rows_in = swap(dispatch(level, ranks, all_tokens, capacity)).reshape(slots, model)
    cotangent = swap(dispatch(level, ranks, all_grads, capacity, gates)).reshape(slots, model)

    hidden, active, slope = hidden_pass(rows_in, w_in, tile)

    def weight_grads(rows, parts):
        return [
            shift(
                dot(rows[:, k * width : (k + 1) * width], parts, ((0,), (0,))).astype(BF16), -k
            )
            for k in range(levels)
        ]

    down_grads = weight_grads(cotangent, hidden)
    expert_out, both = down_pass(hidden, cotangent, active, slope, w_down, tile)
    in_grads = weight_grads(rows_in, both)
    row_grad = row_grad_pass(both, w_in, tile)

    def as_slots(x):
        return x.reshape(wide_count, levels, capacity, model)

    out_parts, dots = combine(level, ranks, swap(as_slots(expert_out)), gates, all_grads)
    layer_output = chain_scatter(out_parts, "narrow", me)
    grad_parts = combine(level, ranks, swap(as_slots(row_grad)))
    token_grad = chain_scatter(grad_parts, "narrow", me)

    gate_parts = jnp.sum(jnp.where(named, dots[:, :, :, None], 0.0), axis=1)
    gate_grad = jnp.sum(
        lax.all_to_all(gate_parts, "narrow", split_axis=0, concat_axis=0, tiled=True), axis=0
    )

    shard = jnp.zeros((levels, width, 3 * units), BF16)
    for k in range(levels):
        spot = lax.rem(me + k, levels)
        shard = lax.dynamic_update_slice(shard, down_grads[k][None], (spot, 0, 2 * units))
    for k in range(levels):
        spot = lax.rem(me + k, levels)
        shard = lax.dynamic_update_slice(shard, in_grads[k][None], (spot, 0, 0))
    weight_shard = jnp.transpose(shard, (1, 0, 2))
    return (layer_output, token_grad, gate_grad, weight_shard)


def solution(mesh):
    return jax.shard_map(
        on_device,
        mesh=mesh,
        in_specs=(
            P(("wide", "narrow"), None),
            P(("wide", "narrow"), None),
            P(("wide", "narrow"), None),
            P(("wide", "narrow"), None),
            P("narrow", "wide", None),
        ),
        out_specs=(
            P(("wide", "narrow"), None),
            P(("wide", "narrow"), None),
            P(("wide", "narrow"), None),
            P("narrow", "wide", None),
        ),
        check_vma=False,
    )
```

```python
import functools

import jax
import jax.numpy as jnp
from jax import lax
from jax.experimental import pallas as pl
from jax.experimental.pallas import tpu as pltpu
from jax.sharding import PartitionSpec as P

F32 = jnp.float32
BF16 = jnp.bfloat16
VMEM_LIMIT = 50 * 1024 * 1024
META = 128
PIECES = 4


def dot(a, b, dims):
    return lax.dot_general(a, b, (dims, ((), ())), preferred_element_type=F32)


def params():
    return pltpu.CompilerParams(vmem_limit_bytes=VMEM_LIMIT)


def whole(shape):
    return pl.BlockSpec(shape, lambda *_: (0,) * len(shape))


def after(x, *others):
    return lax.optimization_barrier((x, others))[0]


def shift(x, k):
    n = lax.axis_size("narrow")
    return lax.ppermute(x, "narrow", [(i, (i + k) % n) for i in range(n)])


def shift_pieces(x, k, pieces, first=()):
    rows = x.shape[0] // pieces
    moved, latest = [], first
    for i in range(pieces):
        moved.append(shift(after(x[i * rows : (i + 1) * rows], *latest), k))
        latest = moved[-1:]
    return jnp.concatenate(moved)


def shift_chain(blocks, sign, order, first=()):
    moved, latest = list(blocks), first
    for k in order:
        moved[k] = shift(after(blocks[k], *latest), sign * k)
        latest = [moved[k]]
    return moved


def hop(x, up, sources):
    step = 1 if up else -1
    return lax.ppermute(x, "narrow", [(i, i + step) for i in sources])


def reduce_chain(parts):
    n = len(parts)
    up = down = None
    for step in range(1, n):
        up_send, down_send = parts[step], parts[n - step]
        if up is not None:
            up_send = (up_send.astype(F32) + up.astype(F32)).astype(BF16)
            down_send = (down_send.astype(F32) + down.astype(F32)).astype(BF16)
        up = hop(up_send, True, range(step))
        down = hop(down_send, False, range(n - step, n))
    total = parts[0].astype(F32) + up.astype(F32) + down.astype(F32)
    return total.astype(BF16)


def mixing(level, n, depth):
    row = lax.broadcasted_iota(jnp.int32, (n * depth, n * depth), 0)
    column = lax.broadcasted_iota(jnp.int32, (n * depth, n * depth), 1)
    same = (row // n == column % depth) & (row % n == lax.rem(level + column // depth, n))
    return jnp.where(same, 1.0, 0.0).astype(BF16)


def split_kernel(n, level_ref, shard_ref, *out_refs):
    depth, _, columns = shard_ref.shape
    part = out_refs[0].shape[1]
    shard = shard_ref[...].reshape(depth * n, columns)
    apart = dot(mixing(level_ref[0], n, depth), shard, ((0,), (0,))).astype(BF16)
    for k in range(n):
        out_refs[k][...] = apart[k * depth : (k + 1) * depth, :part]
        out_refs[n + k][...] = apart[k * depth : (k + 1) * depth, part:]


def split_shard(level, shard, part):
    rows, n, columns = shard.shape
    depth = min(rows, 256 // n)
    rest = columns - part
    outs = pl.pallas_call(
        functools.partial(split_kernel, n),
        out_shape=[jax.ShapeDtypeStruct((rows, part), BF16)] * n
        + [jax.ShapeDtypeStruct((rows, rest), BF16)] * n,
        grid_spec=pltpu.PrefetchScalarGridSpec(
            num_scalar_prefetch=1,
            grid=(rows // depth,),
            in_specs=[pl.BlockSpec((depth, n, columns), lambda i, level: (i, 0, 0))],
            out_specs=[pl.BlockSpec((depth, part), lambda i, level: (i, 0))] * n
            + [pl.BlockSpec((depth, rest), lambda i, level: (i, 0))] * n,
        ),
        compiler_params=params(),
    )(level, shard)
    return outs[:n], outs[n:]


def join_kernel(n, level_ref, *refs):
    out_ref = refs[-1]
    depth, _, columns = out_ref.shape
    apart = jnp.concatenate([ref[...] for ref in refs[:n]], axis=0)
    mixed = dot(mixing(level_ref[0], n, depth), apart, ((1,), (0,)))
    out_ref[...] = mixed.astype(BF16).reshape(depth, n, columns)


def join_shard(level, blocks, columns, place, shard=None):
    n = len(blocks)
    rows, part = blocks[0].shape
    depth = min(rows, 256 // n)
    more = [] if shard is None else [shard]
    return pl.pallas_call(
        functools.partial(join_kernel, n),
        out_shape=jax.ShapeDtypeStruct((rows, n, columns), BF16),
        grid_spec=pltpu.PrefetchScalarGridSpec(
            num_scalar_prefetch=1,
            grid=(rows // depth,),
            in_specs=[pl.BlockSpec((depth, part), lambda i, level: (i, 0))] * n
            + [pl.BlockSpec(memory_space=pl.ANY)] * len(more),
            out_specs=pl.BlockSpec((depth, n, part), lambda i, level: (i, 0, place)),
        ),
        input_output_aliases={1 + n: 0} if more else {},
        compiler_params=params(),
    )(level, *blocks, *more)


def arrived(refs, n, d):
    return refs[0][...] if d == 0 else refs[d][...] + refs[n - 1 + n - d][...]


def slots_of(level, n, groups, chosen, capacity, meta):
    tokens = meta.shape[0]
    lines = jnp.transpose(meta.astype(F32))
    expert = lax.broadcasted_iota(jnp.int32, (groups, tokens), 0) * n + level
    expert = expert.astype(F32)
    named = [lines[k : k + 1] == expert for k in range(chosen)]
    gates = [
        lines[chosen + k : chosen + k + 1]
        + lines[2 * chosen + k : 2 * chosen + k + 1]
        + lines[3 * chosen + k : 3 * chosen + k + 1]
        for k in range(chosen)
    ]
    one = sum(jnp.where(x, 1.0, 0.0) for x in named)
    row = lax.broadcasted_iota(jnp.int32, (tokens, tokens), 0)
    column = lax.broadcasted_iota(jnp.int32, (tokens, tokens), 1)
    earlier = jnp.where(row < column, 1.0, 0.0).astype(BF16)
    rank = dot(one.astype(BF16), earlier, ((1,), (0,)))
    rank = jnp.where(one > 0.5, rank, -1.0).astype(jnp.int32)
    slot = lax.broadcasted_iota(jnp.int32, (groups, capacity, tokens), 1)
    return named, gates, rank[:, None, :] == slot


def gates_of(named, gates):
    return sum(jnp.where(name, gate, 0.0) for name, gate in zip(named, gates))


def dispatch_kernel(n, chosen, gated, level_ref, *refs):
    count = 2 * n - 1
    metas, blocks, out_ref = refs[:count], refs[count : 2 * count], refs[2 * count]
    groups, _, capacity, width = out_ref.shape
    for d in range(n):
        meta, x = arrived(metas, n, d), arrived(blocks, n, d)
        named, gates, taken = slots_of(level_ref[0], n, groups, chosen, capacity, meta)
        tokens = x.shape[0]
        matrix = jnp.where(taken, 1.0, 0.0).astype(BF16).reshape(groups * capacity, tokens)
        rows = dot(matrix, x, ((1,), (0,)))
        if gated:
            weight = jnp.where(taken, gates_of(named, gates)[:, None, :], 0.0)
            weight = jnp.sum(weight, axis=2, keepdims=True)
            rows = rows * weight.reshape(groups * capacity, 1)
        out_ref[:, d] = rows.astype(BF16).reshape(groups, capacity, width)


def rolled(n, tokens, width):
    return pl.BlockSpec((tokens, width), lambda k, level: (0, lax.rem(level[0] - k + n, n)))


def meta_spec(tokens, model):
    return pl.BlockSpec((tokens, META), lambda k, level: (0, model // META))


def dispatch(level, metas, *, blocks, groups, capacity, chosen, gated):
    n = (len(blocks) + 1) // 2
    tokens, model = blocks[0].shape[0], metas[0].shape[1] - META
    width = model // n
    return pl.pallas_call(
        functools.partial(dispatch_kernel, n, chosen, gated),
        out_shape=jax.ShapeDtypeStruct((groups, n, capacity, model), BF16),
        grid_spec=pltpu.PrefetchScalarGridSpec(
            num_scalar_prefetch=1,
            grid=(n,),
            in_specs=[meta_spec(tokens, model)] * len(metas)
            + [rolled(n, tokens, width)] * len(blocks),
            out_specs=pl.BlockSpec((groups, n, capacity, width), lambda k, level: (0, 0, 0, k)),
        ),
        compiler_params=params(),
    )(level, *metas, *blocks)


def combine_out_kernel(n, chosen, level_ref, *refs):
    count = 2 * n - 1
    metas, grads, back_ref = refs[:count], refs[count : 2 * count], refs[2 * count]
    out_refs, dots_ref = refs[2 * count + 1 : -1], refs[-1]
    groups, _, capacity, width = back_ref.shape
    for d in range(n):
        meta, grad = arrived(metas, n, d), arrived(grads, n, d)
        named, gates, taken = slots_of(level_ref[0], n, groups, chosen, capacity, meta)
        tokens = grad.shape[0]
        weight = jnp.where(taken, gates_of(named, gates)[:, None, :], 0.0)
        weight = weight.reshape(groups * capacity, tokens)
        high = weight.astype(BF16)
        low = (weight - high.astype(F32)).astype(BF16)
        rows = back_ref[:, d].reshape(groups * capacity, width)
        total = dot(high, rows, ((0,), (0,))) + dot(low, rows, ((0,), (0,)))
        out_refs[d][...] = total.astype(BF16)
        pairs = dot(rows, grad, ((1,), (1,))).reshape(groups, capacity, tokens)
        pairs = jnp.sum(jnp.where(taken, pairs, 0.0), axis=1)
        part = jnp.concatenate(
            [jnp.sum(jnp.where(name, pairs, 0.0), axis=0, keepdims=True) for name in named]
        )

        @pl.when(pl.program_id(0) == 0)
        def _():
            dots_ref[d] = part

        @pl.when(pl.program_id(0) > 0)
        def _():
            dots_ref[d] += part


def combine_grad_kernel(n, chosen, level_ref, *refs):
    count = 2 * n - 1
    metas, back_ref, out_refs = refs[:count], refs[count], refs[count + 1 :]
    groups, _, capacity, width = back_ref.shape
    for d in range(n):
        meta = arrived(metas, n, d)
        _, _, taken = slots_of(level_ref[0], n, groups, chosen, capacity, meta)
        matrix = jnp.where(taken, 1.0, 0.0).astype(BF16)
        matrix = matrix.reshape(groups * capacity, meta.shape[0])
        rows = back_ref[:, d].reshape(groups * capacity, width)
        out_refs[d][...] = dot(matrix, rows, ((0,), (0,))).astype(BF16)


def combine(level, metas, back, chosen, grads=None):
    groups, n, capacity, model = back.shape
    tokens = metas[0].shape[0]
    width = model // n
    x_spec = rolled(n, tokens, width)
    back_spec = pl.BlockSpec((groups, n, capacity, width), lambda k, level: (0, 0, 0, k))
    out_shape = [jax.ShapeDtypeStruct((tokens, model), BF16)] * n
    out_specs = [x_spec] * n
    in_specs = [meta_spec(tokens, model)] * len(metas)
    if grads is None:
        kernel, extra = combine_grad_kernel, []
    else:
        kernel, extra = combine_out_kernel, grads
        in_specs = in_specs + [x_spec] * len(grads)
        out_shape = out_shape + [jax.ShapeDtypeStruct((n, chosen, tokens), F32)]
        out_specs = out_specs + [whole((n, chosen, tokens))]
    return pl.pallas_call(
        functools.partial(kernel, n, chosen),
        out_shape=out_shape,
        grid_spec=pltpu.PrefetchScalarGridSpec(
            num_scalar_prefetch=1,
            grid=(n,),
            in_specs=in_specs + [back_spec],
            out_specs=out_specs,
        ),
        compiler_params=params(),
    )(level, *metas, *extra, back)


def hidden_kernel(count, *refs):
    rows_ref, weights, outs = refs[0], refs[1 : 1 + count], refs[1 + count :]
    hidden_ref, active_ref, slope_ref = outs
    width = weights[0].shape[0]
    units = hidden_ref.shape[1]
    pre = sum(
        dot(rows_ref[:, k * width : (k + 1) * width], weights[k][...], ((1,), (0,)))
        for k in range(count)
    )
    gate, up = pre[:, :units], pre[:, units:]
    sigmoid = jax.nn.sigmoid(gate)
    active = gate * sigmoid
    hidden_ref[...] = (active * up).astype(BF16)
    active_ref[...] = active
    slope_ref[...] = up * (sigmoid * (1.0 + gate * (1.0 - sigmoid)))


def hidden_pass(rows, weights, tile):
    slots, model = rows.shape
    units = weights[0].shape[1] // 2
    out_spec = pl.BlockSpec((tile, units), lambda i: (i, 0))
    return pl.pallas_call(
        functools.partial(hidden_kernel, len(weights)),
        out_shape=(
            jax.ShapeDtypeStruct((slots, units), BF16),
            jax.ShapeDtypeStruct((slots, units), F32),
            jax.ShapeDtypeStruct((slots, units), F32),
        ),
        grid=(slots // tile,),
        in_specs=[pl.BlockSpec((tile, model), lambda i: (i, 0))]
        + [whole(w.shape) for w in weights],
        out_specs=(out_spec, out_spec, out_spec),
        compiler_params=params(),
    )(rows, *weights)


def down_kernel(count, *refs):
    hidden_ref, cotangent_ref, active_ref, slope_ref = refs[:4]
    weights = refs[4 : 4 + count]
    out_ref, both_ref = refs[4 + count :]
    width = weights[0].shape[0]
    hidden = hidden_ref[...]
    units = hidden.shape[1]
    grad = None
    for k in range(count):
        weight = weights[k][...]
        out_ref[:, k * width : (k + 1) * width] = dot(hidden, weight, ((1,), (1,))).astype(BF16)
        part = dot(cotangent_ref[:, k * width : (k + 1) * width], weight, ((1,), (0,)))
        grad = part if grad is None else grad + part
    both_ref[:, :units] = (grad * slope_ref[...]).astype(BF16)
    both_ref[:, units:] = (grad * active_ref[...]).astype(BF16)


def down_pass(hidden, cotangent, active, slope, weights, tile):
    slots, model = cotangent.shape
    units = hidden.shape[1]
    unit_spec = pl.BlockSpec((tile, units), lambda i: (i, 0))
    model_spec = pl.BlockSpec((tile, model), lambda i: (i, 0))
    return pl.pallas_call(
        functools.partial(down_kernel, len(weights)),
        out_shape=(
            jax.ShapeDtypeStruct((slots, model), BF16),
            jax.ShapeDtypeStruct((slots, 2 * units), BF16),
        ),
        grid=(slots // tile,),
        in_specs=[unit_spec, model_spec, unit_spec, unit_spec]
        + [whole(w.shape) for w in weights],
        out_specs=(model_spec, pl.BlockSpec((tile, 2 * units), lambda i: (i, 0))),
        compiler_params=params(),
    )(hidden, cotangent, active, slope, *weights)


def row_grad_kernel(count, *refs):
    both_ref, weights, out_ref = refs[0], refs[1 : 1 + count], refs[1 + count]
    width = weights[0].shape[0]
    for k in range(count):
        out_ref[:, k * width : (k + 1) * width] = dot(
            both_ref[...], weights[k][...], ((1,), (1,))
        ).astype(BF16)


def row_grad_pass(both, weights, tile):
    slots, units = both.shape
    model = len(weights) * weights[0].shape[0]
    return pl.pallas_call(
        functools.partial(row_grad_kernel, len(weights)),
        out_shape=jax.ShapeDtypeStruct((slots, model), BF16),
        grid=(slots // tile,),
        in_specs=[pl.BlockSpec((tile, units), lambda i: (i, 0))]
        + [whole(w.shape) for w in weights],
        out_specs=pl.BlockSpec((tile, model), lambda i: (i, 0)),
        compiler_params=params(),
    )(both, *weights)


def weight_grad_kernel(rows_ref, parts_ref, out_ref):
    out_ref[...] = dot(rows_ref[...], parts_ref[...], ((0,), (0,))).astype(BF16)


def weight_grad(rows, parts, k, width):
    slots, columns = parts.shape
    tile = columns // 2 if columns % 256 == 0 else columns
    return pl.pallas_call(
        weight_grad_kernel,
        out_shape=jax.ShapeDtypeStruct((width, columns), BF16),
        grid=(columns // tile,),
        in_specs=[
            pl.BlockSpec((slots, width), lambda i: (0, k)),
            pl.BlockSpec((slots, tile), lambda i: (0, i)),
        ],
        out_specs=pl.BlockSpec((width, tile), lambda i: (0, i)),
        compiler_params=params(),
    )(rows, parts)


def on_device(tokens, out_grad, routes, route_gates, expert_weights):
    groups = lax.axis_size("wide")
    n = lax.axis_size("narrow")
    me = lax.axis_index("narrow")
    experts = groups * n
    token_count, model = tokens.shape
    chosen = routes.shape[1]
    capacity = 2 * chosen * token_count // experts
    slots = experts * capacity
    width = model // n
    units = expert_weights.shape[2] // 3
    level = me.astype(jnp.int32).reshape(1)
    tile = min(256, slots)

    high = route_gates.astype(BF16)
    rest = route_gates - high.astype(F32)
    middle = rest.astype(BF16)
    low = (rest - middle.astype(F32)).astype(BF16)
    pad = jnp.zeros((token_count, META - 4 * chosen), BF16)
    sent = jnp.concatenate([tokens, routes.astype(BF16), high, middle, low, pad], axis=1)
    in_blocks, down_blocks = split_shard(level, expert_weights, 2 * units)
    middle, others = n // 2, [k for k in range(1, n) if k != n // 2]

    def swap(x):
        return lax.all_to_all(x, "wide", split_axis=0, concat_axis=0, tiled=True)

    def as_slots(x):
        return x.reshape(groups, n, capacity, model)

    w_in = [in_blocks[0]] + [None] * (n - 1)
    token_up, token_down = [sent], [sent]
    stage = list(in_blocks)
    for step in range(1, n):
        up, down = token_up[-1], token_down[-1]
        if step > 1:
            up, down = after((up, down), *stage)
            k = others[step - 2]
            w_in[k] = shift(after(in_blocks[k], token_up[-1], token_down[-1], *stage), k)
            stage = [w_in[k]]
        token_up.append(hop(up, True, range(step - 1, n - 1)))
        token_down.append(hop(down, False, range(1, n - step + 1)))
    token_blocks = token_up + token_down[1:]
    stage = stage + [token_up[-1], token_down[-1]]

    place = functools.partial(
        dispatch, level, groups=groups, capacity=capacity, chosen=chosen
    )
    sent_rows = place(after(token_blocks, *stage), blocks=token_blocks, gated=False)
    w_in[middle] = shift_pieces(in_blocks[middle], middle, PIECES, stage)
    start = after(out_grad, *stage)
    grad_up, grad_down = [start], [start]
    for step in range(1, n):
        grad_up.append(hop(grad_up[-1], True, range(step - 1, n - 1)))
        grad_down.append(hop(grad_down[-1], False, range(1, n - step + 1)))
    grad_blocks = grad_up + grad_down[1:]
    rows_in = swap(sent_rows).reshape(slots, model)
    stage = [w_in[middle], grad_up[-1], grad_down[-1]]

    w_down = shift_chain(down_blocks, 1, others + [middle], stage)
    sent_grads = place(after(token_blocks, *stage), blocks=grad_blocks, gated=True)
    cotangent = swap(sent_grads).reshape(slots, model)
    hidden, active, slope = hidden_pass(rows_in, w_in, tile)
    down_grads = [weight_grad(cotangent, hidden, k, width) for k in range(n)]
    stage = w_down + down_grads

    hidden = after(hidden, *stage)
    down_grads = shift_chain(down_grads, -1, others + [middle], stage)
    expert_out, both = down_pass(hidden, cotangent, active, slope, w_down, tile)
    in_grads = [weight_grad(rows_in, both, k, width) for k in range(n)]
    both = after(both, *in_grads)
    row_grad = row_grad_pass(both, w_in, tile)
    back_out = swap(as_slots(expert_out))
    stage = down_grads + [back_out, row_grad]
    columns = 3 * units
    shard = join_shard(level, down_grads, columns, 2)

    in_grads[middle] = shift_pieces(in_grads[middle], -middle, PIECES, stage)
    back_grad = swap(as_slots(after(row_grad, *stage)))
    back_out = after(back_out, *stage)
    *out_parts, dots = combine(level, token_blocks, back_out, chosen, grad_blocks)
    layer_output = reduce_chain(out_parts)
    stage = [in_grads[middle], layer_output, back_grad]
    for k in others:
        in_grads[k] = shift_pieces(in_grads[k], -k, PIECES // 2, stage)
        stage = [in_grads[k]]
    grad_parts = combine(level, token_blocks, after(back_grad, shard, layer_output), chosen)
    token_grad = reduce_chain(grad_parts)
    gate_grad = dots[0] + sum(shift(dots[d], -d) for d in range(1, n))

    shard = join_shard(level, in_grads, columns, 0, shard)
    return (layer_output, token_grad, gate_grad.T, shard)


def solution(mesh):
    return jax.shard_map(
        on_device,
        mesh=mesh,
        in_specs=(
            P(("wide", "narrow"), None),
            P(("wide", "narrow"), None),
            P(("wide", "narrow"), None),
            P(("wide", "narrow"), None),
            P("narrow", "wide", None),
        ),
        out_specs=(
            P(("wide", "narrow"), None),
            P(("wide", "narrow"), None),
            P(("wide", "narrow"), None),
            P("narrow", "wide", None),
        ),
        check_vma=False,
    )
```

```python
import functools

import jax
import jax.numpy as jnp
from jax import lax
from jax.experimental import pallas as pl
from jax.experimental.pallas import tpu as pltpu
from jax.sharding import PartitionSpec as P

F32 = jnp.float32
BF16 = jnp.bfloat16
VMEM_LIMIT = 50 * 1024 * 1024
META = 128
LANES = 2
FLOPS_PER_VALUE = 40000


def dot(a, b, dims):
    return lax.dot_general(a, b, (dims, ((), ())), preferred_element_type=F32)


def params():
    return pltpu.CompilerParams(vmem_limit_bytes=VMEM_LIMIT)


def whole(shape):
    return pl.BlockSpec(shape, lambda *_: (0,) * len(shape))


def after(x, *others):
    return lax.optimization_barrier((x, others))[0]


def shift(x, k):
    n = lax.axis_size("narrow")
    return lax.ppermute(x, "narrow", [(i, (i + k) % n) for i in range(n)])


def arrival_kernel(moved_ref, out_ref, done_ref):
    done_ref[...] = jnp.zeros_like(done_ref)


def arrival(moved, load):
    anywhere = pl.BlockSpec(memory_space=pl.ANY)
    return pl.pallas_call(
        arrival_kernel,
        out_shape=jax.ShapeDtypeStruct(moved.shape, moved.dtype),
        in_specs=[anywhere],
        out_specs=anywhere,
        scratch_shapes=[pltpu.VMEM((8, 128), F32)],
        input_output_aliases={0: 0},
        cost_estimate=pl.CostEstimate(
            flops=FLOPS_PER_VALUE * moved.size * load, bytes_accessed=0, transcendentals=0
        ),
    )(moved)


class Lanes:
    def __init__(self, count, first):
        self.latest = [first] * count
        self.sent = []

    def send(self, x, k, others=()):
        lane = len(self.sent) % len(self.latest)
        n = lax.axis_size("narrow")
        moved = shift(after(x, self.latest[lane], others), k)
        moved = arrival(moved, min(k % n, -k % n))
        self.latest[lane] = moved
        self.sent.append(moved)
        return moved

    def send_all(self, blocks, sign, order, others=()):
        waits = iter(others)
        return {
            k: [self.send(x, sign * k, next(waits, ())) if k else x for x in blocks[k]]
            for k in order
        }

    def done(self, i):
        return self.sent[min(i, len(self.sent) - 1)]


def hop(x, up, sources):
    step = 1 if up else -1
    return lax.ppermute(x, "narrow", [(i, i + step) for i in sources])


def reduce_chain(parts):
    n = len(parts)
    up = down = None
    steps = []
    for step in range(1, n):
        up_send, down_send = parts[step], parts[n - step]
        if up is not None:
            up_send = (up_send.astype(F32) + up.astype(F32)).astype(BF16)
            down_send = (down_send.astype(F32) + down.astype(F32)).astype(BF16)
        up = hop(up_send, True, range(step))
        down = hop(down_send, False, range(n - step, n))
        steps.append((up, down))
    total = parts[0].astype(F32) + up.astype(F32) + down.astype(F32)
    return total.astype(BF16), steps


def mixing(level, n, depth):
    row = lax.broadcasted_iota(jnp.int32, (n * depth, n * depth), 0)
    column = lax.broadcasted_iota(jnp.int32, (n * depth, n * depth), 1)
    same = (row // n == column % depth) & (row % n == lax.rem(level + column // depth, n))
    return jnp.where(same, 1.0, 0.0).astype(BF16)


def split_kernel(n, level_ref, shard_ref, *out_refs):
    depth, _, columns = shard_ref.shape
    part = out_refs[0].shape[1]
    shard = shard_ref[...].reshape(depth * n, columns)
    apart = dot(mixing(level_ref[0], n, depth), shard, ((0,), (0,))).astype(BF16)
    for i, out_ref in enumerate(out_refs):
        k, group = i % n, i // n
        out_ref[...] = apart[k * depth : (k + 1) * depth, group * part : (group + 1) * part]


def split_shard(level, shard, part):
    rows, n, columns = shard.shape
    depth = min(rows, 256 // n)
    count = columns // part
    outs = pl.pallas_call(
        functools.partial(split_kernel, n),
        out_shape=[jax.ShapeDtypeStruct((rows, part), BF16)] * (n * count),
        grid_spec=pltpu.PrefetchScalarGridSpec(
            num_scalar_prefetch=1,
            grid=(rows // depth,),
            in_specs=[pl.BlockSpec((depth, n, columns), lambda i, level: (i, 0, 0))],
            out_specs=[pl.BlockSpec((depth, part), lambda i, level: (i, 0))] * (n * count),
        ),
        compiler_params=params(),
    )(level, shard)
    return [outs[i * n : (i + 1) * n] for i in range(count)]


def join_kernel(n, level_ref, *refs):
    out_ref = refs[-1]
    depth, _, columns = out_ref.shape
    apart = jnp.concatenate([ref[...] for ref in refs[:n]], axis=0)
    mixed = dot(mixing(level_ref[0], n, depth), apart, ((1,), (0,)))
    out_ref[...] = mixed.astype(BF16).reshape(depth, n, columns)


def join_shard(level, blocks, columns, place, shard=None):
    n = len(blocks)
    rows, part = blocks[0].shape
    depth = min(rows, 256 // n)
    more = [] if shard is None else [shard]
    return pl.pallas_call(
        functools.partial(join_kernel, n),
        out_shape=jax.ShapeDtypeStruct((rows, n, columns), BF16),
        grid_spec=pltpu.PrefetchScalarGridSpec(
            num_scalar_prefetch=1,
            grid=(rows // depth,),
            in_specs=[pl.BlockSpec((depth, part), lambda i, level: (i, 0))] * n
            + [pl.BlockSpec(memory_space=pl.ANY)] * len(more),
            out_specs=pl.BlockSpec((depth, n, part), lambda i, level: (i, 0, place)),
        ),
        input_output_aliases={1 + n: 0} if more else {},
        compiler_params=params(),
    )(level, *blocks, *more)


def arrived(refs, n, d):
    return refs[0][...] if d == 0 else refs[d][...] + refs[n - 1 + n - d][...]


def slots_of(level, n, groups, chosen, capacity, meta):
    tokens = meta.shape[0]
    lines = jnp.transpose(meta.astype(F32))
    expert = lax.broadcasted_iota(jnp.int32, (groups, tokens), 0) * n + level
    expert = expert.astype(F32)
    named = [lines[k : k + 1] == expert for k in range(chosen)]
    gates = [
        lines[chosen + k : chosen + k + 1]
        + lines[2 * chosen + k : 2 * chosen + k + 1]
        + lines[3 * chosen + k : 3 * chosen + k + 1]
        for k in range(chosen)
    ]
    one = sum(jnp.where(x, 1.0, 0.0) for x in named)
    row = lax.broadcasted_iota(jnp.int32, (tokens, tokens), 0)
    column = lax.broadcasted_iota(jnp.int32, (tokens, tokens), 1)
    earlier = jnp.where(row < column, 1.0, 0.0).astype(BF16)
    rank = dot(one.astype(BF16), earlier, ((1,), (0,)))
    rank = jnp.where(one > 0.5, rank, -1.0).astype(jnp.int32)
    slot = lax.broadcasted_iota(jnp.int32, (groups, capacity, tokens), 1)
    return named, gates, rank[:, None, :] == slot


def gates_of(named, gates):
    return sum(jnp.where(name, gate, 0.0) for name, gate in zip(named, gates))


def dispatch_kernel(n, chosen, gated, level_ref, *refs):
    count = 2 * n - 1
    metas, blocks, out_ref = refs[:count], refs[count : 2 * count], refs[2 * count]
    groups, _, capacity, width = out_ref.shape
    for d in range(n):
        meta, x = arrived(metas, n, d), arrived(blocks, n, d)
        named, gates, taken = slots_of(level_ref[0], n, groups, chosen, capacity, meta)
        tokens = x.shape[0]
        matrix = jnp.where(taken, 1.0, 0.0).astype(BF16).reshape(groups * capacity, tokens)
        rows = dot(matrix, x, ((1,), (0,)))
        if gated:
            weight = jnp.where(taken, gates_of(named, gates)[:, None, :], 0.0)
            weight = jnp.sum(weight, axis=2, keepdims=True)
            rows = rows * weight.reshape(groups * capacity, 1)
        out_ref[:, d] = rows.astype(BF16).reshape(groups, capacity, width)


def rolled(n, tokens, width):
    return pl.BlockSpec((tokens, width), lambda k, level: (0, lax.rem(level[0] - k + n, n)))


def meta_spec(tokens, model):
    return pl.BlockSpec((tokens, META), lambda k, level: (0, model // META))


def dispatch(level, metas, *, blocks, groups, capacity, chosen, gated):
    n = (len(blocks) + 1) // 2
    tokens, model = blocks[0].shape[0], metas[0].shape[1] - META
    width = model // n
    return pl.pallas_call(
        functools.partial(dispatch_kernel, n, chosen, gated),
        out_shape=jax.ShapeDtypeStruct((groups, n, capacity, model), BF16),
        grid_spec=pltpu.PrefetchScalarGridSpec(
            num_scalar_prefetch=1,
            grid=(n,),
            in_specs=[meta_spec(tokens, model)] * len(metas)
            + [rolled(n, tokens, width)] * len(blocks),
            out_specs=pl.BlockSpec((groups, n, capacity, width), lambda k, level: (0, 0, 0, k)),
        ),
        compiler_params=params(),
    )(level, *metas, *blocks)


def combine_out_kernel(n, chosen, level_ref, *refs):
    count = 2 * n - 1
    metas, grads, back_ref = refs[:count], refs[count : 2 * count], refs[2 * count]
    out_refs, dots_ref = refs[2 * count + 1 : -1], refs[-1]
    groups, _, capacity, width = back_ref.shape
    for d in range(n):
        meta, grad = arrived(metas, n, d), arrived(grads, n, d)
        named, gates, taken = slots_of(level_ref[0], n, groups, chosen, capacity, meta)
        tokens = grad.shape[0]
        weight = jnp.where(taken, gates_of(named, gates)[:, None, :], 0.0)
        weight = weight.reshape(groups * capacity, tokens)
        high = weight.astype(BF16)
        low = (weight - high.astype(F32)).astype(BF16)
        rows = back_ref[:, d].reshape(groups * capacity, width)
        total = dot(high, rows, ((0,), (0,))) + dot(low, rows, ((0,), (0,)))
        out_refs[d][...] = total.astype(BF16)
        pairs = dot(rows, grad, ((1,), (1,))).reshape(groups, capacity, tokens)
        pairs = jnp.sum(jnp.where(taken, pairs, 0.0), axis=1)
        part = jnp.concatenate(
            [jnp.sum(jnp.where(name, pairs, 0.0), axis=0, keepdims=True) for name in named]
        )

        @pl.when(pl.program_id(0) == 0)
        def _():
            dots_ref[d] = part

        @pl.when(pl.program_id(0) > 0)
        def _():
            dots_ref[d] += part


def combine_grad_kernel(n, chosen, level_ref, *refs):
    count = 2 * n - 1
    metas, back_ref, out_refs = refs[:count], refs[count], refs[count + 1 :]
    groups, _, capacity, width = back_ref.shape
    for d in range(n):
        meta = arrived(metas, n, d)
        _, _, taken = slots_of(level_ref[0], n, groups, chosen, capacity, meta)
        matrix = jnp.where(taken, 1.0, 0.0).astype(BF16)
        matrix = matrix.reshape(groups * capacity, meta.shape[0])
        rows = back_ref[:, d].reshape(groups * capacity, width)
        out_refs[d][...] = dot(matrix, rows, ((0,), (0,))).astype(BF16)


def combine(level, metas, back, chosen, grads=None):
    groups, n, capacity, model = back.shape
    tokens = metas[0].shape[0]
    width = model // n
    x_spec = rolled(n, tokens, width)
    back_spec = pl.BlockSpec((groups, n, capacity, width), lambda k, level: (0, 0, 0, k))
    out_shape = [jax.ShapeDtypeStruct((tokens, model), BF16)] * n
    out_specs = [x_spec] * n
    in_specs = [meta_spec(tokens, model)] * len(metas)
    if grads is None:
        kernel, extra = combine_grad_kernel, []
    else:
        kernel, extra = combine_out_kernel, grads
        in_specs = in_specs + [x_spec] * len(grads)
        out_shape = out_shape + [jax.ShapeDtypeStruct((n, chosen, tokens), F32)]
        out_specs = out_specs + [whole((n, chosen, tokens))]
    return pl.pallas_call(
        functools.partial(kernel, n, chosen),
        out_shape=out_shape,
        grid_spec=pltpu.PrefetchScalarGridSpec(
            num_scalar_prefetch=1,
            grid=(n,),
            in_specs=in_specs + [back_spec],
            out_specs=out_specs,
        ),
        compiler_params=params(),
    )(level, *metas, *extra, back)


def spans(weights):
    start = 0
    for weight in weights:
        yield weight, slice(start, start + weight.shape[0])
        start += weight.shape[0]


def times(rows_ref, weights):
    return sum(dot(rows_ref[:, span], w[...], ((1,), (0,))) for w, span in spans(weights))


def hidden_kernel(count, *refs):
    rows_ref, gates, ups = refs[0], refs[1 : 1 + count], refs[1 + count : 1 + 2 * count]
    hidden_ref, active_ref, slope_ref = refs[1 + 2 * count :]
    gate, up = times(rows_ref, gates), times(rows_ref, ups)
    sigmoid = jax.nn.sigmoid(gate)
    active = gate * sigmoid
    hidden_ref[...] = (active * up).astype(BF16)
    active_ref[...] = active
    slope_ref[...] = up * (sigmoid * (1.0 + gate * (1.0 - sigmoid)))


def hidden_pass(rows, gates, ups, tile):
    slots, model = rows.shape
    units = gates[0].shape[1]
    out_spec = pl.BlockSpec((tile, units), lambda i: (i, 0))
    return pl.pallas_call(
        functools.partial(hidden_kernel, len(gates)),
        out_shape=(
            jax.ShapeDtypeStruct((slots, units), BF16),
            jax.ShapeDtypeStruct((slots, units), F32),
            jax.ShapeDtypeStruct((slots, units), F32),
        ),
        grid=(slots // tile,),
        in_specs=[pl.BlockSpec((tile, model), lambda i: (i, 0))]
        + [whole(w.shape) for w in gates + ups],
        out_specs=(out_spec, out_spec, out_spec),
        compiler_params=params(),
    )(rows, *gates, *ups)


def down_kernel(count, *refs):
    hidden_ref, cotangent_ref, active_ref, slope_ref = refs[:4]
    downs = refs[4 : 4 + count]
    out_ref, gate_ref, up_ref = refs[4 + count :]
    hidden = hidden_ref[...]
    for weight, span in spans(downs):
        out_ref[:, span] = dot(hidden, weight[...], ((1,), (1,))).astype(BF16)
    grad = times(cotangent_ref, downs)
    gate_ref[...] = (grad * slope_ref[...]).astype(BF16)
    up_ref[...] = (grad * active_ref[...]).astype(BF16)


def down_pass(hidden, cotangent, active, slope, downs, tile):
    slots, model = cotangent.shape
    units = hidden.shape[1]
    unit_spec = pl.BlockSpec((tile, units), lambda i: (i, 0))
    model_spec = pl.BlockSpec((tile, model), lambda i: (i, 0))
    return pl.pallas_call(
        functools.partial(down_kernel, len(downs)),
        out_shape=(
            jax.ShapeDtypeStruct((slots, model), BF16),
            jax.ShapeDtypeStruct((slots, units), BF16),
            jax.ShapeDtypeStruct((slots, units), BF16),
        ),
        grid=(slots // tile,),
        in_specs=[unit_spec, model_spec, unit_spec, unit_spec]
        + [whole(w.shape) for w in downs],
        out_specs=(model_spec, unit_spec, unit_spec),
        compiler_params=params(),
    )(hidden, cotangent, active, slope, *downs)


def row_grad_kernel(count, *refs):
    gate_ref, up_ref = refs[:2]
    gates, ups, out_ref = refs[2 : 2 + count], refs[2 + count : 2 + 2 * count], refs[-1]
    for (gate, span), up in zip(spans(gates), ups):
        total = dot(gate_ref[...], gate[...], ((1,), (1,)))
        total += dot(up_ref[...], up[...], ((1,), (1,)))
        out_ref[:, span] = total.astype(BF16)


def row_grad_pass(gate_part, up_part, gates, ups, tile):
    slots, units = gate_part.shape
    model = sum(w.shape[0] for w in gates)
    unit_spec = pl.BlockSpec((tile, units), lambda i: (i, 0))
    return pl.pallas_call(
        functools.partial(row_grad_kernel, len(gates)),
        out_shape=jax.ShapeDtypeStruct((slots, model), BF16),
        grid=(slots // tile,),
        in_specs=[unit_spec, unit_spec] + [whole(w.shape) for w in gates + ups],
        out_specs=pl.BlockSpec((tile, model), lambda i: (i, 0)),
        compiler_params=params(),
    )(gate_part, up_part, *gates, *ups)


def weight_grad_kernel(rows_ref, *refs):
    half = len(refs) // 2
    for part_ref, out_ref in zip(refs[:half], refs[half:]):
        out_ref[...] = dot(rows_ref[...], part_ref[...], ((0,), (0,))).astype(BF16)


def weight_grad(rows, parts, place, width):
    slots, columns = parts[0].shape
    tile = columns // 2 if columns % 256 == 0 else columns
    count = len(parts)
    return pl.pallas_call(
        weight_grad_kernel,
        out_shape=[jax.ShapeDtypeStruct((width, columns), BF16)] * count,
        grid=(columns // tile,),
        in_specs=[pl.BlockSpec((slots, width), lambda i: (0, place))]
        + [pl.BlockSpec((slots, tile), lambda i: (0, i))] * count,
        out_specs=[pl.BlockSpec((width, tile), lambda i: (0, i))] * count,
        compiler_params=params(),
    )(rows, *parts)


def on_device(tokens, out_grad, routes, route_gates, expert_weights):
    groups = lax.axis_size("wide")
    n = lax.axis_size("narrow")
    me = lax.axis_index("narrow")
    experts = groups * n
    token_count, model = tokens.shape
    chosen = routes.shape[1]
    capacity = 2 * chosen * token_count // experts
    slots = experts * capacity
    width = model // n
    units = expert_weights.shape[2] // 3
    level = me.astype(jnp.int32).reshape(1)
    tile = min(256, slots)

    high = lax.reduce_precision(route_gates, 8, 7)
    middle = lax.reduce_precision(route_gates - high, 8, 7)
    low = route_gates - high - middle
    thirds = [x.astype(BF16) for x in (high, middle, low)]
    pad = jnp.zeros((token_count, META - 4 * chosen), BF16)
    sent = jnp.concatenate([tokens, routes.astype(BF16), *thirds, pad], axis=1)
    middle = n // 2
    order = [k for k in range(1, n) if k != middle] + [middle, 0]

    def halves(k):
        return 2 if k == middle else 1

    def pieces(blocks):
        return [jnp.split(x, halves(k)) for k, x in enumerate(blocks)]

    def in_order(moved):
        return [x for k in range(n) for x in moved[k]]

    def swap(x):
        return lax.all_to_all(x, "wide", split_axis=0, concat_axis=0, tiled=True)

    def as_slots(x):
        return x.reshape(groups, n, capacity, model)

    gate_blocks, up_blocks, down_blocks = split_shard(level, expert_weights, units)

    def hop_on(ups, downs, *others):
        step = len(ups)
        up, down = after((ups[-1], downs[-1]), others)
        ups.append(hop(up, True, range(step - 1, n - 1)))
        downs.append(hop(down, False, range(1, n - step + 1)))

    token_up, token_down, grad_up, grad_down = [sent], [sent], [out_grad], [out_grad]
    hop_on(token_up, token_down)
    lanes = Lanes(LANES, (token_up[1], token_down[1]))
    for step in range(2, n):
        hop_on(token_up, token_down, gate_blocks if step == 2 else ())
    for step in range(1, n):
        hop_on(grad_up, grad_down, token_up[1], token_down[1])
    token_blocks = token_up + token_down[1:]
    grad_blocks = grad_up + grad_down[1:]

    def both_ways(ups, downs, step):
        return ups[min(step, n - 1)], downs[min(step, n - 1)]

    tokens_at = functools.partial(both_ways, token_up, token_down)
    grads_at = functools.partial(both_ways, grad_up, grad_down)
    waits = ((), (), (), tokens_at(2), grads_at(1), tokens_at(n - 1), grads_at(2), grads_at(n - 1))
    gates = in_order(lanes.send_all(pieces(gate_blocks), 1, order, waits[:4]))
    ups = in_order(lanes.send_all(pieces(up_blocks), 1, order, waits[4:]))

    place = functools.partial(
        dispatch, level, token_blocks, groups=groups, capacity=capacity, chosen=chosen
    )
    rows_in = swap(place(blocks=token_blocks, gated=False)).reshape(slots, model)
    cotangent = swap(place(blocks=grad_blocks, gated=True)).reshape(slots, model)
    hidden, active, slope = hidden_pass(rows_in, gates, ups, tile)
    waits = (rows_in, (), hidden, cotangent)
    downs = in_order(lanes.send_all(pieces(down_blocks), 1, order, waits))

    def weight_grads(rows, *parts):
        made = [
            [
                weight_grad(rows, parts, k * halves(k) + i, width // halves(k))
                for i in range(halves(k))
            ]
            for k in range(n)
        ]
        return [[[x[j] for x in blocks] for blocks in made] for j in range(len(parts))]

    def send_back(blocks, others=()):
        moved, waits = {0: blocks[0]}, list(others)
        for k in order[:-1]:
            moved[k] = []
            for x in blocks[k]:
                wait = waits.pop(0) if waits else ()
                moved[k].append(lanes.send(x, -k, wait() if callable(wait) else wait))
        return [jnp.concatenate(moved[k]) if halves(k) > 1 else moved[k][0] for k in range(n)]

    (down_grads,) = weight_grads(cotangent, hidden)
    hidden = after(hidden, down_grads)
    first = len(lanes.sent)
    down_grads = send_back(down_grads)
    expert_out, gate_part, up_part = down_pass(hidden, cotangent, active, slope, downs, tile)
    back_out = swap(as_slots(after(expert_out, lanes.done(first))))
    gate_grads, up_grads = weight_grads(
        rows_in, after(gate_part, lanes.done(first + 1)), up_part
    )
    row_grad = row_grad_pass(
        after(gate_part, gate_grads, lanes.done(first + 2)), up_part, gates, ups, tile
    )
    back_grad = swap(as_slots(after(row_grad, back_out)))

    sums = {}

    def sum_outputs():
        back = after(back_out, lanes.done(first + 4))
        *parts, sums["dots"] = combine(level, token_blocks, back, chosen, grad_blocks)
        sums["output"], sums["steps"] = reduce_chain(parts)
        return parts

    gate_grads = send_back(gate_grads, ((), row_grad, (), sum_outputs))
    layer_output, out_steps, dots = sums["output"], sums["steps"], sums["dots"]
    gate_grad = dots[0] + sum(shift(dots[d], -d) for d in range(1, n))
    grad_parts = combine(
        level, token_blocks, after(back_grad, lanes.done(first + 6)), chosen
    )
    token_grad, grad_steps = reduce_chain(grad_parts)
    up_grads = send_back(
        up_grads,
        (
            (out_steps[0], back_grad),
            (out_steps[1], grad_parts),
            (out_steps[-1], grad_steps[0]),
            (grad_steps[1], gate_grad),
        ),
    )

    columns = 3 * units
    shard = join_shard(level, after(down_grads, lanes.done(first + 7)), columns, 2)
    shard = join_shard(level, after(gate_grads, lanes.done(first + 9)), columns, 0, shard)
    shard = join_shard(level, up_grads, columns, 1, shard)
    return (layer_output, token_grad, gate_grad.T, shard)


def solution(mesh):
    return jax.shard_map(
        on_device,
        mesh=mesh,
        in_specs=(
            P(("wide", "narrow"), None),
            P(("wide", "narrow"), None),
            P(("wide", "narrow"), None),
            P(("wide", "narrow"), None),
            P("narrow", "wide", None),
        ),
        out_specs=(
            P(("wide", "narrow"), None),
            P(("wide", "narrow"), None),
            P(("wide", "narrow"), None),
            P("narrow", "wide", None),
        ),
        check_vma=False,
    )
```

```python
import functools

import jax
import jax.numpy as jnp
from jax import lax
from jax.experimental import pallas as pl
from jax.experimental.pallas import tpu as pltpu
from jax.sharding import PartitionSpec as P

F32 = jnp.float32
BF16 = jnp.bfloat16
VMEM_LIMIT = 50 * 1024 * 1024
META = 128
LANES = 2
FLOPS_PER_VALUE = 40000
BACK_TURNS = (2, 0, 1)
MIDDLE_FIRST = (False, False)
WAITS = {3: ['t2'],
 4: ['g1'],
 5: ['t3'],
 6: ['g2'],
 7: ['g3'],
 10: ['units_pass', 'cotangent'],
 12: ['middle_down_grad', 'own_down_grad', 'other_down_grads'],
 17: ['row_grad'],
 18: ['back_out'],
 19: ['out_parts'],
 20: ['o1'],
 21: ['o2', 'back_grad'],
 22: ['o3', 'grad_parts', 'gate_grad']}
GATES = {'back_out': [12],
 'down': ['other_down_grads', 'middle_down_grad', 'own_down_grad'],
 'g1': ['t1'],
 'grad_parts': [19],
 'join0': [19],
 'join1': [21],
 'middle_in_grad': ['row_grad'],
 'other_in_grads': [13],
 'out_sums': [16],
 'own_in_grad': [18],
 'row_grad': ['other_in_grads', 14],
 't2': ['split']}


def dot(a, b, dims):
    return lax.dot_general(a, b, (dims, ((), ())), preferred_element_type=F32)


def params():
    return pltpu.CompilerParams(vmem_limit_bytes=VMEM_LIMIT)


def whole(shape):
    return pl.BlockSpec(shape, lambda *_: (0,) * len(shape))


def after(x, *others):
    return lax.optimization_barrier((x, others))[0]


def shift(x, k):
    n = lax.axis_size("narrow")
    return lax.ppermute(x, "narrow", [(i, (i + k) % n) for i in range(n)])


def arrival_kernel(moved_ref, out_ref, done_ref):
    done_ref[...] = jnp.zeros_like(done_ref)


def arrival(moved, load):
    anywhere = pl.BlockSpec(memory_space=pl.ANY)
    return pl.pallas_call(
        arrival_kernel,
        out_shape=jax.ShapeDtypeStruct(moved.shape, moved.dtype),
        in_specs=[anywhere],
        out_specs=anywhere,
        scratch_shapes=[pltpu.VMEM((8, 128), F32)],
        input_output_aliases={0: 0},
        cost_estimate=pl.CostEstimate(
            flops=FLOPS_PER_VALUE * moved.size * load, bytes_accessed=0, transcendentals=0
        ),
    )(moved)


class Lanes:
    def __init__(self, count, first):
        self.latest = [first] * count
        self.sent = []

    def send(self, x, k, others=()):
        lane = len(self.sent) % len(self.latest)
        n = lax.axis_size("narrow")
        moved = shift(after(x, self.latest[lane], others), k)
        moved = arrival(moved, min(k % n, -k % n))
        self.latest[lane] = moved
        self.sent.append(moved)
        return moved


class Parts:
    def __init__(self):
        self.made = {}

    def __call__(self, name):
        if name not in self.made:
            self.made[name] = getattr(self, name)()
        return self.made[name]


def hop(x, up, sources):
    step = 1 if up else -1
    return lax.ppermute(x, "narrow", [(i, i + step) for i in sources])


def reduce_step(parts, last, step):
    n = len(parts)
    up_send, down_send = parts[step], parts[n - step]
    if last is not None:
        up_send = (up_send.astype(F32) + last[0].astype(F32)).astype(BF16)
        down_send = (down_send.astype(F32) + last[1].astype(F32)).astype(BF16)
    return hop(up_send, True, range(step)), hop(down_send, False, range(n - step, n))


def reduce_end(parts, last):
    total = parts[0].astype(F32) + last[0].astype(F32) + last[1].astype(F32)
    return total.astype(BF16)


def mixing(level, n, depth):
    row = lax.broadcasted_iota(jnp.int32, (n * depth, n * depth), 0)
    column = lax.broadcasted_iota(jnp.int32, (n * depth, n * depth), 1)
    same = (row // n == column % depth) & (row % n == lax.rem(level + column // depth, n))
    return jnp.where(same, 1.0, 0.0).astype(BF16)


def split_kernel(n, level_ref, shard_ref, *out_refs):
    depth, _, columns = shard_ref.shape
    part = out_refs[0].shape[1]
    shard = shard_ref[...].reshape(depth * n, columns)
    apart = dot(mixing(level_ref[0], n, depth), shard, ((0,), (0,))).astype(BF16)
    for i, out_ref in enumerate(out_refs):
        k, group = i % n, i // n
        out_ref[...] = apart[k * depth : (k + 1) * depth, group * part : (group + 1) * part]


def split_shard(level, shard, part):
    rows, n, columns = shard.shape
    depth = min(rows, 256 // n)
    count = columns // part
    outs = pl.pallas_call(
        functools.partial(split_kernel, n),
        out_shape=[jax.ShapeDtypeStruct((rows, part), BF16)] * (n * count),
        grid_spec=pltpu.PrefetchScalarGridSpec(
            num_scalar_prefetch=1,
            grid=(rows // depth,),
            in_specs=[pl.BlockSpec((depth, n, columns), lambda i, level: (i, 0, 0))],
            out_specs=[pl.BlockSpec((depth, part), lambda i, level: (i, 0))] * (n * count),
        ),
        compiler_params=params(),
    )(level, shard)
    return [outs[i * n : (i + 1) * n] for i in range(count)]


def join_kernel(n, level_ref, *refs):
    out_ref = refs[-1]
    depth, _, columns = out_ref.shape
    apart = jnp.concatenate([ref[...] for ref in refs[:n]], axis=0)
    mixed = dot(mixing(level_ref[0], n, depth), apart, ((1,), (0,)))
    out_ref[...] = mixed.astype(BF16).reshape(depth, n, columns)


def join_shard(level, blocks, columns, place, shard=None):
    n = len(blocks)
    rows, part = blocks[0].shape
    depth = min(rows, 256 // n)
    more = [] if shard is None else [shard]
    return pl.pallas_call(
        functools.partial(join_kernel, n),
        out_shape=jax.ShapeDtypeStruct((rows, n, columns), BF16),
        grid_spec=pltpu.PrefetchScalarGridSpec(
            num_scalar_prefetch=1,
            grid=(rows // depth,),
            in_specs=[pl.BlockSpec((depth, part), lambda i, level: (i, 0))] * n
            + [pl.BlockSpec(memory_space=pl.ANY)] * len(more),
            out_specs=pl.BlockSpec((depth, n, part), lambda i, level: (i, 0, place)),
        ),
        input_output_aliases={1 + n: 0} if more else {},
        compiler_params=params(),
    )(level, *blocks, *more)


def arrived(refs, n, d):
    return refs[0][...] if d == 0 else refs[d][...] + refs[n - 1 + n - d][...]


def slots_of(level, n, groups, chosen, capacity, meta):
    tokens = meta.shape[0]
    lines = jnp.transpose(meta.astype(F32))
    expert = lax.broadcasted_iota(jnp.int32, (groups, tokens), 0) * n + level
    expert = expert.astype(F32)
    named = [lines[k : k + 1] == expert for k in range(chosen)]
    gates = [
        lines[chosen + k : chosen + k + 1]
        + lines[2 * chosen + k : 2 * chosen + k + 1]
        + lines[3 * chosen + k : 3 * chosen + k + 1]
        for k in range(chosen)
    ]
    one = sum(jnp.where(x, 1.0, 0.0) for x in named)
    row = lax.broadcasted_iota(jnp.int32, (tokens, tokens), 0)
    column = lax.broadcasted_iota(jnp.int32, (tokens, tokens), 1)
    earlier = jnp.where(row < column, 1.0, 0.0).astype(BF16)
    rank = dot(one.astype(BF16), earlier, ((1,), (0,)))
    rank = jnp.where(one > 0.5, rank, -1.0).astype(jnp.int32)
    slot = lax.broadcasted_iota(jnp.int32, (groups, capacity, tokens), 1)
    return named, gates, rank[:, None, :] == slot


def gates_of(named, gates):
    return sum(jnp.where(name, gate, 0.0) for name, gate in zip(named, gates))


def dispatch_kernel(n, chosen, gated, level_ref, *refs):
    count = 2 * n - 1
    metas, blocks, out_ref = refs[:count], refs[count : 2 * count], refs[2 * count]
    groups, _, capacity, width = out_ref.shape
    for d in range(n):
        meta, x = arrived(metas, n, d), arrived(blocks, n, d)
        named, gates, taken = slots_of(level_ref[0], n, groups, chosen, capacity, meta)
        tokens = x.shape[0]
        matrix = jnp.where(taken, 1.0, 0.0).astype(BF16).reshape(groups * capacity, tokens)
        rows = dot(matrix, x, ((1,), (0,)))
        if gated:
            weight = jnp.where(taken, gates_of(named, gates)[:, None, :], 0.0)
            weight = jnp.sum(weight, axis=2, keepdims=True)
            rows = rows * weight.reshape(groups * capacity, 1)
        out_ref[:, d] = rows.astype(BF16).reshape(groups, capacity, width)


def rolled(n, tokens, width):
    return pl.BlockSpec((tokens, width), lambda k, level: (0, lax.rem(level[0] - k + n, n)))


def meta_spec(tokens, model):
    return pl.BlockSpec((tokens, META), lambda k, level: (0, model // META))


def dispatch(level, metas, *, blocks, groups, capacity, chosen, gated):
    n = (len(blocks) + 1) // 2
    tokens, model = blocks[0].shape[0], metas[0].shape[1] - META
    width = model // n
    return pl.pallas_call(
        functools.partial(dispatch_kernel, n, chosen, gated),
        out_shape=jax.ShapeDtypeStruct((groups, n, capacity, model), BF16),
        grid_spec=pltpu.PrefetchScalarGridSpec(
            num_scalar_prefetch=1,
            grid=(n,),
            in_specs=[meta_spec(tokens, model)] * len(metas)
            + [rolled(n, tokens, width)] * len(blocks),
            out_specs=pl.BlockSpec((groups, n, capacity, width), lambda k, level: (0, 0, 0, k)),
        ),
        compiler_params=params(),
    )(level, *metas, *blocks)


def combine_out_kernel(n, chosen, level_ref, *refs):
    count = 2 * n - 1
    metas, grads, back_ref = refs[:count], refs[count : 2 * count], refs[2 * count]
    out_refs, dots_ref = refs[2 * count + 1 : -1], refs[-1]
    groups, _, capacity, width = back_ref.shape
    for d in range(n):
        meta, grad = arrived(metas, n, d), arrived(grads, n, d)
        named, gates, taken = slots_of(level_ref[0], n, groups, chosen, capacity, meta)
        tokens = grad.shape[0]
        weight = jnp.where(taken, gates_of(named, gates)[:, None, :], 0.0)
        weight = weight.reshape(groups * capacity, tokens)
        high = weight.astype(BF16)
        low = (weight - high.astype(F32)).astype(BF16)
        rows = back_ref[:, d].reshape(groups * capacity, width)
        total = dot(high, rows, ((0,), (0,))) + dot(low, rows, ((0,), (0,)))
        out_refs[d][...] = total.astype(BF16)
        pairs = dot(rows, grad, ((1,), (1,))).reshape(groups, capacity, tokens)
        pairs = jnp.sum(jnp.where(taken, pairs, 0.0), axis=1)
        part = jnp.concatenate(
            [jnp.sum(jnp.where(name, pairs, 0.0), axis=0, keepdims=True) for name in named]
        )

        @pl.when(pl.program_id(0) == 0)
        def _():
            dots_ref[d] = part

        @pl.when(pl.program_id(0) > 0)
        def _():
            dots_ref[d] += part


def combine_grad_kernel(n, chosen, level_ref, *refs):
    count = 2 * n - 1
    metas, back_ref, out_refs = refs[:count], refs[count], refs[count + 1 :]
    groups, _, capacity, width = back_ref.shape
    for d in range(n):
        meta = arrived(metas, n, d)
        _, _, taken = slots_of(level_ref[0], n, groups, chosen, capacity, meta)
        matrix = jnp.where(taken, 1.0, 0.0).astype(BF16)
        matrix = matrix.reshape(groups * capacity, meta.shape[0])
        rows = back_ref[:, d].reshape(groups * capacity, width)
        out_refs[d][...] = dot(matrix, rows, ((0,), (0,))).astype(BF16)


def combine(level, metas, back, chosen, grads=None):
    groups, n, capacity, model = back.shape
    tokens = metas[0].shape[0]
    width = model // n
    x_spec = rolled(n, tokens, width)
    back_spec = pl.BlockSpec((groups, n, capacity, width), lambda k, level: (0, 0, 0, k))
    out_shape = [jax.ShapeDtypeStruct((tokens, model), BF16)] * n
    out_specs = [x_spec] * n
    in_specs = [meta_spec(tokens, model)] * len(metas)
    if grads is None:
        kernel, extra = combine_grad_kernel, []
    else:
        kernel, extra = combine_out_kernel, grads
        in_specs = in_specs + [x_spec] * len(grads)
        out_shape = out_shape + [jax.ShapeDtypeStruct((n, chosen, tokens), F32)]
        out_specs = out_specs + [whole((n, chosen, tokens))]
    return pl.pallas_call(
        functools.partial(kernel, n, chosen),
        out_shape=out_shape,
        grid_spec=pltpu.PrefetchScalarGridSpec(
            num_scalar_prefetch=1,
            grid=(n,),
            in_specs=in_specs + [back_spec],
            out_specs=out_specs,
        ),
        compiler_params=params(),
    )(level, *metas, *extra, back)


def spans(weights):
    start = 0
    for weight in weights:
        yield weight, slice(start, start + weight.shape[0])
        start += weight.shape[0]


def times(rows_ref, weights):
    return sum(dot(rows_ref[:, span], w[...], ((1,), (0,))) for w, span in spans(weights))


def hidden_kernel(count, *refs):
    rows_ref, gates, ups = refs[0], refs[1 : 1 + count], refs[1 + count : 1 + 2 * count]
    hidden_ref, active_ref, slope_ref = refs[1 + 2 * count :]
    gate, up = times(rows_ref, gates), times(rows_ref, ups)
    sigmoid = jax.nn.sigmoid(gate)
    active = gate * sigmoid
    hidden_ref[...] = (active * up).astype(BF16)
    active_ref[...] = active
    slope_ref[...] = up * (sigmoid * (1.0 + gate * (1.0 - sigmoid)))


def hidden_pass(rows, gates, ups, tile):
    slots, model = rows.shape
    units = gates[0].shape[1]
    out_spec = pl.BlockSpec((tile, units), lambda i: (i, 0))
    return pl.pallas_call(
        functools.partial(hidden_kernel, len(gates)),
        out_shape=(
            jax.ShapeDtypeStruct((slots, units), BF16),
            jax.ShapeDtypeStruct((slots, units), F32),
            jax.ShapeDtypeStruct((slots, units), F32),
        ),
        grid=(slots // tile,),
        in_specs=[pl.BlockSpec((tile, model), lambda i: (i, 0))]
        + [whole(w.shape) for w in gates + ups],
        out_specs=(out_spec, out_spec, out_spec),
        compiler_params=params(),
    )(rows, *gates, *ups)


def down_kernel(count, *refs):
    hidden_ref, cotangent_ref, active_ref, slope_ref = refs[:4]
    downs = refs[4 : 4 + count]
    out_ref, gate_ref, up_ref = refs[4 + count :]
    hidden = hidden_ref[...]
    for weight, span in spans(downs):
        out_ref[:, span] = dot(hidden, weight[...], ((1,), (1,))).astype(BF16)
    grad = times(cotangent_ref, downs)
    gate_ref[...] = (grad * slope_ref[...]).astype(BF16)
    up_ref[...] = (grad * active_ref[...]).astype(BF16)


def down_pass(hidden, cotangent, active, slope, downs, tile):
    slots, model = cotangent.shape
    units = hidden.shape[1]
    unit_spec = pl.BlockSpec((tile, units), lambda i: (i, 0))
    model_spec = pl.BlockSpec((tile, model), lambda i: (i, 0))
    return pl.pallas_call(
        functools.partial(down_kernel, len(downs)),
        out_shape=(
            jax.ShapeDtypeStruct((slots, model), BF16),
            jax.ShapeDtypeStruct((slots, units), BF16),
            jax.ShapeDtypeStruct((slots, units), BF16),
        ),
        grid=(slots // tile,),
        in_specs=[unit_spec, model_spec, unit_spec, unit_spec]
        + [whole(w.shape) for w in downs],
        out_specs=(model_spec, unit_spec, unit_spec),
        compiler_params=params(),
    )(hidden, cotangent, active, slope, *downs)


def row_grad_kernel(count, *refs):
    gate_ref, up_ref = refs[:2]
    gates, ups, out_ref = refs[2 : 2 + count], refs[2 + count : 2 + 2 * count], refs[-1]
    for (gate, span), up in zip(spans(gates), ups):
        total = dot(gate_ref[...], gate[...], ((1,), (1,)))
        total += dot(up_ref[...], up[...], ((1,), (1,)))
        out_ref[:, span] = total.astype(BF16)


def row_grad_pass(gate_part, up_part, gates, ups, tile):
    slots, units = gate_part.shape
    model = sum(w.shape[0] for w in gates)
    unit_spec = pl.BlockSpec((tile, units), lambda i: (i, 0))
    return pl.pallas_call(
        functools.partial(row_grad_kernel, len(gates)),
        out_shape=jax.ShapeDtypeStruct((slots, model), BF16),
        grid=(slots // tile,),
        in_specs=[unit_spec, unit_spec] + [whole(w.shape) for w in gates + ups],
        out_specs=pl.BlockSpec((tile, model), lambda i: (i, 0)),
        compiler_params=params(),
    )(gate_part, up_part, *gates, *ups)


def weight_grad_kernel(rows_ref, *refs):
    half = len(refs) // 2
    for part_ref, out_ref in zip(refs[:half], refs[half:]):
        out_ref[...] = dot(rows_ref[...], part_ref[...], ((0,), (0,))).astype(BF16)


def weight_grad(rows, parts, place, width):
    slots, columns = parts[0].shape
    tile = columns // 2 if columns % 256 == 0 else columns
    count = len(parts)
    return pl.pallas_call(
        weight_grad_kernel,
        out_shape=[jax.ShapeDtypeStruct((width, columns), BF16)] * count,
        grid=(columns // tile,),
        in_specs=[pl.BlockSpec((slots, width), lambda i: (0, place))]
        + [pl.BlockSpec((slots, tile), lambda i: (0, i))] * count,
        out_specs=[pl.BlockSpec((width, tile), lambda i: (0, i))] * count,
        compiler_params=params(),
    )(rows, *parts)


def on_device(tokens, out_grad, routes, route_gates, expert_weights):
    groups = lax.axis_size("wide")
    n = lax.axis_size("narrow")
    me = lax.axis_index("narrow")
    experts = groups * n
    token_count, model = tokens.shape
    chosen = routes.shape[1]
    capacity = 2 * chosen * token_count // experts
    slots = experts * capacity
    width = model // n
    units = expert_weights.shape[2] // 3
    level = me.astype(jnp.int32).reshape(1)
    tile = min(256, slots)

    high = lax.reduce_precision(route_gates, 8, 7)
    middle = lax.reduce_precision(route_gates - high, 8, 7)
    low = route_gates - high - middle
    thirds = [x.astype(BF16) for x in (high, middle, low)]
    pad = jnp.zeros((token_count, META - 4 * chosen), BF16)
    sent = jnp.concatenate([tokens, routes.astype(BF16), *thirds, pad], axis=1)
    middle = n // 2
    others = [k for k in range(1, n) if k != middle]
    blocks = split_shard(level, expert_weights, units)
    lanes = Lanes(LANES, ())

    def halves(k):
        return 2 if k == middle else 1

    def swap(x):
        x = x.reshape(groups, n, capacity, model)
        return lax.all_to_all(x, "wide", split_axis=0, concat_axis=0, tiled=True)

    def place(x, gated):
        token_blocks = part("token_blocks")
        return dispatch(
            level, token_blocks, blocks=x, groups=groups, capacity=capacity, chosen=chosen, gated=gated
        )

    def gated(name, x):
        waits = [
            part(y) if isinstance(y, str) else lanes.sent[y * n // 4] for y in GATES.get(name, ())
        ]
        return after(x, *waits) if waits else x

    def hop_on(ups, downs, name):
        step = len(ups)
        up, down = gated(name, (ups[-1], downs[-1]))
        ups.append(hop(up, True, range(step - 1, n - 1)))
        downs.append(hop(down, False, range(1, n - step + 1)))

    def moved(group):
        return [x for k in range(n) for x in came[group][k]]

    came = [{0: [x[0]]} for x in blocks] + [{} for _ in blocks]
    part = Parts()
    steps = [n - 1 if i == 3 else i * (n - 1) // 3 for i in range(4)]
    lines = {"t": ([sent], [sent]), "g": ([out_grad], [out_grad])}

    def line_part(letter, i):
        def make():
            if i > 1:
                part(f"{letter}{i - 1}")
            ups, downs = lines[letter]
            while len(ups) <= steps[i]:
                hop_on(ups, downs, f"{letter}{i}")
            return ups[-1], downs[-1]

        return make

    def sum_part(letter, i):
        def make():
            last = part(f"{letter}{i - 1}") if i > 1 else None
            parts = part("out_parts" if letter == "o" else "grad_parts")
            for step in range(steps[i - 1] + 1, steps[i] + 1):
                last = reduce_step(parts, last, step)
            return last

        return make

    for i in (1, 2, 3):
        for letter in "tg":
            setattr(part, f"{letter}{i}", line_part(letter, i))
        for letter in "or":
            setattr(part, f"{letter}{i}", sum_part(letter, i))

    def define(make):
        setattr(part, make.__name__, make)

    @define
    def split():
        return blocks

    @define
    def token_blocks():
        part("t3")
        return lines["t"][0] + lines["t"][1][1:]

    @define
    def grad_blocks():
        part("g3")
        return lines["g"][0] + lines["g"][1][1:]

    @define
    def rows():
        return swap(place(part("token_blocks"), False)).reshape(slots, model)

    @define
    def cotangent():
        return swap(place(part("grad_blocks"), True)).reshape(slots, model)

    @define
    def units_pass():
        return hidden_pass(gated("units_pass", part("rows")), moved(0), moved(1), tile)

    def grad_pieces(k, rows, *parts):
        made = [
            weight_grad(rows, parts, k * halves(k) + i, width // halves(k))
            for i in range(halves(k))
        ]
        return [[x[j] for x in made] for j in range(len(parts))]

    def down_grad(k, name):
        return grad_pieces(k, part("cotangent"), gated(name, part("units_pass")[0]))[0]

    def in_grad(k, name):
        _, gate_part, up_part = part("down")
        return grad_pieces(k, part("rows"), gated(name, gate_part), up_part)

    @define
    def middle_down_grad():
        return {middle: down_grad(middle, "middle_down_grad")}

    @define
    def other_down_grads():
        return {k: down_grad(k, "other_down_grads") for k in others}

    @define
    def own_down_grad():
        return {0: down_grad(0, "own_down_grad")}

    @define
    def down():
        hidden, active, slope = part("units_pass")
        return down_pass(gated("down", hidden), part("cotangent"), active, slope, moved(2), tile)

    @define
    def middle_in_grad():
        return {middle: in_grad(middle, "middle_in_grad")}

    @define
    def other_in_grads():
        return {k: in_grad(k, "other_in_grads") for k in others}

    @define
    def own_in_grad():
        return {0: in_grad(0, "own_in_grad")}

    @define
    def row_grad():
        _, gate_part, up_part = part("down")
        return row_grad_pass(gated("row_grad", gate_part), up_part, moved(0), moved(1), tile)

    @define
    def back_out():
        return swap(gated("back_out", part("down")[0]))

    @define
    def back_grad():
        return swap(gated("back_grad", after(part("row_grad"), part("back_out"))))

    @define
    def out_sums():
        back = gated("out_sums", part("back_out"))
        return combine(level, part("token_blocks"), back, chosen, part("grad_blocks"))

    @define
    def out_parts():
        return part("out_sums")[:-1]

    @define
    def grad_parts():
        return combine(level, part("token_blocks"), gated("grad_parts", part("back_grad")), chosen)

    @define
    def gate_grad():
        dots = gated("gate_grad", part("out_sums")[-1])
        return dots[0] + sum(shift(dots[d], -d) for d in range(1, n))

    def joined(group, name, shard=None):
        grads = [part(own)[0] for own in ("own_down_grad",)] if group == 2 else None
        if grads is None:
            grads = [part("own_in_grad")[0][group]]
        grads = [jnp.concatenate(x) for x in grads]
        grads += [jnp.concatenate(came[3 + group][k]) for k in range(1, n)]
        return join_shard(level, gated(name, grads), 3 * units, group, shard)

    def pieces_of(group, back, k):
        if not back:
            return jnp.split(blocks[group][k], halves(k))
        name = "middle" if k == middle else "other"
        if group == 2:
            return part("middle_down_grad" if k == middle else "other_down_grads")[k]
        return part("middle_in_grad" if k == middle else "other_in_grads")[k][group]

    part("t1")
    lanes.latest = [part("t1")] * LANES
    for back, turns in ((False, (0, 1, 2)), (True, BACK_TURNS)):
        for group in turns:
            order = [middle, *others] if MIDDLE_FIRST[back] else [*others, middle]
            for k in order:
                arrived = came[group + (3 if back else 0)].setdefault(k, [])
                for i in range(halves(k)):
                    names = WAITS.get(len(lanes.sent) * 4 // n, ())
                    names = names if len(lanes.sent) % max(1, n // 4) == 0 else ()
                    waits = [part(name) for name in names]
                    x = pieces_of(group, back, k)[i]
                    arrived.append(lanes.send(x, -k if back else k, waits))
    layer_output = reduce_end(part("out_parts"), part("o3"))
    token_grad = reduce_end(part("grad_parts"), part("r3"))
    shard = None
    for i, group in enumerate(BACK_TURNS):
        shard = joined(group, f"join{i}", shard)
    return (layer_output, token_grad, part("gate_grad").T, shard)


def solution(mesh):
    return jax.shard_map(
        on_device,
        mesh=mesh,
        in_specs=(
            P(("wide", "narrow"), None),
            P(("wide", "narrow"), None),
            P(("wide", "narrow"), None),
            P(("wide", "narrow"), None),
            P("narrow", "wide", None),
        ),
        out_specs=(
            P(("wide", "narrow"), None),
            P(("wide", "narrow"), None),
            P(("wide", "narrow"), None),
            P("narrow", "wide", None),
        ),
        check_vma=False,
    )
```

```python
import functools

import jax
import jax.numpy as jnp
from jax import lax
from jax.experimental import pallas as pl
from jax.experimental.pallas import tpu as pltpu
from jax.sharding import PartitionSpec as P

F32 = jnp.float32
BF16 = jnp.bfloat16
VMEM_LIMIT = 50 * 1024 * 1024
META = 128
LANES = 2
FLOPS_PER_VALUE = 40000
BACK_TURNS = (2, 0, 1)
MIDDLE_FIRST = (False, False)
WAITS = {3: ['t2'],
 4: ['g1'],
 5: ['t3'],
 6: ['g2'],
 7: ['g3'],
 10: ['units_pass', 'cotangent'],
 12: ['middle_down_grad', 'own_down_grad', 'other_down_grads'],
 17: ['row_grad'],
 18: ['back_out'],
 19: ['out_parts'],
 20: ['o1'],
 21: ['o2', 'back_grad'],
 22: ['o3', 'grad_parts', 'gate_grad']}
GATES = {'back_out': [12],
 'down': ['other_down_grads', 'middle_down_grad', 'own_down_grad'],
 'g1': ['t1'],
 'grad_parts': [19],
 'join0': [19],
 'join1': [21],
 'middle_in_grad': [16],
 'other_in_grads': [13],
 'out_sums': [16],
 'own_in_grad': [18],
 'row_grad': ['other_in_grads', 14],
 't2': ['split']}


def dot(a, b, dims):
    return lax.dot_general(a, b, (dims, ((), ())), preferred_element_type=F32)


def params():
    return pltpu.CompilerParams(vmem_limit_bytes=VMEM_LIMIT)


def whole(shape):
    return pl.BlockSpec(shape, lambda *_: (0,) * len(shape))


def after(x, *others):
    return lax.optimization_barrier((x, others))[0]


def shift(x, k):
    n = lax.axis_size("narrow")
    return lax.ppermute(x, "narrow", [(i, (i + k) % n) for i in range(n)])


def arrival_kernel(moved_ref, out_ref, done_ref):
    done_ref[...] = jnp.zeros_like(done_ref)


def arrival(moved, load):
    anywhere = pl.BlockSpec(memory_space=pl.ANY)
    return pl.pallas_call(
        arrival_kernel,
        out_shape=jax.ShapeDtypeStruct(moved.shape, moved.dtype),
        in_specs=[anywhere],
        out_specs=anywhere,
        scratch_shapes=[pltpu.VMEM((8, 128), F32)],
        input_output_aliases={0: 0},
        cost_estimate=pl.CostEstimate(
            flops=FLOPS_PER_VALUE * moved.size * load, bytes_accessed=0, transcendentals=0
        ),
    )(moved)


class Lanes:
    def __init__(self, count, first):
        self.latest = [first] * count
        self.sent = []

    def send(self, x, k, others=()):
        lane = len(self.sent) % len(self.latest)
        n = lax.axis_size("narrow")
        moved = shift(after(x, self.latest[lane], others), k)
        moved = arrival(moved, min(k % n, -k % n))
        self.latest[lane] = moved
        self.sent.append(moved)
        return moved


class Parts:
    def __init__(self):
        self.made = {}

    def __call__(self, name):
        if name not in self.made:
            self.made[name] = getattr(self, name)()
        return self.made[name]


def hop(x, up, sources):
    step = 1 if up else -1
    return lax.ppermute(x, "narrow", [(i, i + step) for i in sources])


def reduce_step(parts, last, step):
    n = len(parts)
    up_send, down_send = parts[step], parts[n - step]
    if last is not None:
        up_send = (up_send.astype(F32) + last[0].astype(F32)).astype(BF16)
        down_send = (down_send.astype(F32) + last[1].astype(F32)).astype(BF16)
    return hop(up_send, True, range(step)), hop(down_send, False, range(n - step, n))


def reduce_end(parts, last):
    total = parts[0].astype(F32) + last[0].astype(F32) + last[1].astype(F32)
    return total.astype(BF16)


def mixing(level, n, depth):
    row = lax.broadcasted_iota(jnp.int32, (n * depth, n * depth), 0)
    column = lax.broadcasted_iota(jnp.int32, (n * depth, n * depth), 1)
    same = (row // n == column % depth) & (row % n == lax.rem(level + column // depth, n))
    return jnp.where(same, 1.0, 0.0).astype(BF16)


def split_kernel(n, level_ref, shard_ref, *out_refs):
    depth, _, columns = shard_ref.shape
    part = out_refs[0].shape[1]
    shard = shard_ref[...].reshape(depth * n, columns)
    apart = dot(mixing(level_ref[0], n, depth), shard, ((0,), (0,))).astype(BF16)
    for i, out_ref in enumerate(out_refs):
        k, group = i % n, i // n
        out_ref[...] = apart[k * depth : (k + 1) * depth, group * part : (group + 1) * part]


def split_shard(level, shard, part):
    rows, n, columns = shard.shape
    depth = min(rows, 256 // n)
    count = columns // part
    outs = pl.pallas_call(
        functools.partial(split_kernel, n),
        out_shape=[jax.ShapeDtypeStruct((rows, part), BF16)] * (n * count),
        grid_spec=pltpu.PrefetchScalarGridSpec(
            num_scalar_prefetch=1,
            grid=(rows // depth,),
            in_specs=[pl.BlockSpec((depth, n, columns), lambda i, level: (i, 0, 0))],
            out_specs=[pl.BlockSpec((depth, part), lambda i, level: (i, 0))] * (n * count),
        ),
        compiler_params=params(),
    )(level, shard)
    return [outs[i * n : (i + 1) * n] for i in range(count)]


def join_kernel(n, level_ref, *refs):
    out_ref = refs[-1]
    depth, _, columns = out_ref.shape
    apart = jnp.concatenate([ref[...] for ref in refs[:n]], axis=0)
    mixed = dot(mixing(level_ref[0], n, depth), apart, ((1,), (0,)))
    out_ref[...] = mixed.astype(BF16).reshape(depth, n, columns)


def join_shard(level, blocks, columns, place, shard=None):
    n = len(blocks)
    rows, part = blocks[0].shape
    depth = min(rows, 256 // n)
    more = [] if shard is None else [shard]
    return pl.pallas_call(
        functools.partial(join_kernel, n),
        out_shape=jax.ShapeDtypeStruct((rows, n, columns), BF16),
        grid_spec=pltpu.PrefetchScalarGridSpec(
            num_scalar_prefetch=1,
            grid=(rows // depth,),
            in_specs=[pl.BlockSpec((depth, part), lambda i, level: (i, 0))] * n
            + [pl.BlockSpec(memory_space=pl.ANY)] * len(more),
            out_specs=pl.BlockSpec((depth, n, part), lambda i, level: (i, 0, place)),
        ),
        input_output_aliases={1 + n: 0} if more else {},
        compiler_params=params(),
    )(level, *blocks, *more)


def arrived(refs, n, d):
    return refs[0][...] if d == 0 else refs[d][...] + refs[n - 1 + n - d][...]


def slots_of(level, n, groups, chosen, capacity, meta):
    tokens = meta.shape[0]
    lines = jnp.transpose(meta.astype(F32))
    expert = lax.broadcasted_iota(jnp.int32, (groups, tokens), 0) * n + level
    expert = expert.astype(F32)
    named = [lines[k : k + 1] == expert for k in range(chosen)]
    gates = [
        lines[chosen + k : chosen + k + 1]
        + lines[2 * chosen + k : 2 * chosen + k + 1]
        + lines[3 * chosen + k : 3 * chosen + k + 1]
        for k in range(chosen)
    ]
    one = sum(jnp.where(x, 1.0, 0.0) for x in named)
    row = lax.broadcasted_iota(jnp.int32, (tokens, tokens), 0)
    column = lax.broadcasted_iota(jnp.int32, (tokens, tokens), 1)
    earlier = jnp.where(row < column, 1.0, 0.0).astype(BF16)
    rank = dot(one.astype(BF16), earlier, ((1,), (0,)))
    rank = jnp.where(one > 0.5, rank, -1.0).astype(jnp.int32)
    slot = lax.broadcasted_iota(jnp.int32, (groups, capacity, tokens), 1)
    return named, gates, rank[:, None, :] == slot


def gates_of(named, gates):
    return sum(jnp.where(name, gate, 0.0) for name, gate in zip(named, gates))


def dispatch_kernel(n, chosen, gated, level_ref, *refs):
    count = 2 * n - 1
    metas, blocks, out_ref = refs[:count], refs[count : 2 * count], refs[2 * count]
    matrix_ref, weight_ref = refs[2 * count + 1 :]
    groups, _, capacity, width = out_ref.shape

    @pl.when(pl.program_id(0) == 0)
    def _():
        for d in range(n):
            meta = arrived(metas, n, d)
            tokens = meta.shape[0]
            named, gates, taken = slots_of(level_ref[0], n, groups, chosen, capacity, meta)
            matrix = jnp.where(taken, 1.0, 0.0).astype(BF16)
            matrix_ref[d] = matrix.reshape(groups * capacity, tokens)
            if gated:
                weight = jnp.where(taken, gates_of(named, gates)[:, None, :], 0.0)
                weight = jnp.sum(weight, axis=2, keepdims=True)
                weight_ref[d] = weight.reshape(groups * capacity, 1)

    for d in range(n):
        rows = dot(matrix_ref[d], arrived(blocks, n, d), ((1,), (0,)))
        if gated:
            rows = rows * weight_ref[d]
        out_ref[:, d] = rows.astype(BF16).reshape(groups, capacity, width)


def rolled(n, tokens, width):
    return pl.BlockSpec((tokens, width), lambda k, level: (0, lax.rem(level[0] - k + n, n)))


def meta_spec(tokens, model):
    return pl.BlockSpec((tokens, META), lambda k, level: (0, model // META))


def dispatch(level, metas, *, blocks, groups, capacity, chosen, gated):
    n = (len(blocks) + 1) // 2
    tokens, model = blocks[0].shape[0], metas[0].shape[1] - META
    width = model // n
    return pl.pallas_call(
        functools.partial(dispatch_kernel, n, chosen, gated),
        out_shape=jax.ShapeDtypeStruct((groups, n, capacity, model), BF16),
        grid_spec=pltpu.PrefetchScalarGridSpec(
            num_scalar_prefetch=1,
            grid=(n,),
            in_specs=[meta_spec(tokens, model)] * len(metas)
            + [rolled(n, tokens, width)] * len(blocks),
            out_specs=pl.BlockSpec((groups, n, capacity, width), lambda k, level: (0, 0, 0, k)),
            scratch_shapes=[
                pltpu.VMEM((n, groups * capacity, tokens), BF16),
                pltpu.VMEM((n, groups * capacity, 1), F32),
            ],
        ),
        compiler_params=params(),
    )(level, *metas, *blocks)


def combine_out_kernel(n, chosen, level_ref, *refs):
    count = 2 * n - 1
    metas, grads, back_ref = refs[:count], refs[count : 2 * count], refs[2 * count]
    out_refs, dots_ref = refs[2 * count + 1 : 2 * count + 1 + n], refs[2 * count + 1 + n]
    matrix_ref, high_ref, low_ref, pairs_ref = refs[2 * count + 2 + n :]
    groups, _, capacity, width = back_ref.shape
    tokens = metas[0].shape[0]
    step = pl.program_id(0)

    def slots(d):
        return slots_of(level_ref[0], n, groups, chosen, capacity, arrived(metas, n, d))

    @pl.when(step == 0)
    def _():
        for d in range(n):
            named, gates, taken = slots(d)
            weight = jnp.where(taken, gates_of(named, gates)[:, None, :], 0.0)
            weight = weight.reshape(groups * capacity, tokens)
            high = weight.astype(BF16)
            high_ref[d] = high
            low_ref[d] = (weight - high.astype(F32)).astype(BF16)
            matrix = jnp.where(taken, 1.0, 0.0)
            matrix_ref[d] = matrix.reshape(groups * capacity, tokens)
        pairs_ref[...] = jnp.zeros_like(pairs_ref)

    for d in range(n):
        rows = back_ref[:, d].reshape(groups * capacity, width)
        total = dot(high_ref[d], rows, ((0,), (0,))) + dot(low_ref[d], rows, ((0,), (0,)))
        out_refs[d][...] = total.astype(BF16)
        pairs_ref[d] += dot(rows, arrived(grads, n, d), ((1,), (1,)))

    @pl.when(step == n - 1)
    def _():
        for d in range(n):
            named, _, _ = slots(d)
            pairs = pairs_ref[d] * matrix_ref[d]
            pairs = jnp.sum(pairs.reshape(groups, capacity, tokens), axis=1)
            dots_ref[d] = jnp.concatenate(
                [jnp.sum(jnp.where(name, pairs, 0.0), axis=0, keepdims=True) for name in named]
            )


def combine_grad_kernel(n, chosen, level_ref, *refs):
    count = 2 * n - 1
    metas, back_ref, out_refs = refs[:count], refs[count], refs[count + 1 : count + 1 + n]
    matrix_ref = refs[count + 1 + n]
    groups, _, capacity, width = back_ref.shape
    tokens = metas[0].shape[0]

    @pl.when(pl.program_id(0) == 0)
    def _():
        for d in range(n):
            meta = arrived(metas, n, d)
            _, _, taken = slots_of(level_ref[0], n, groups, chosen, capacity, meta)
            matrix = jnp.where(taken, 1.0, 0.0).astype(BF16)
            matrix_ref[d] = matrix.reshape(groups * capacity, tokens)

    for d in range(n):
        rows = back_ref[:, d].reshape(groups * capacity, width)
        out_refs[d][...] = dot(matrix_ref[d], rows, ((0,), (0,))).astype(BF16)


def combine(level, metas, back, chosen, grads=None):
    groups, n, capacity, model = back.shape
    tokens = metas[0].shape[0]
    width = model // n
    x_spec = rolled(n, tokens, width)
    back_spec = pl.BlockSpec((groups, n, capacity, width), lambda k, level: (0, 0, 0, k))
    out_shape = [jax.ShapeDtypeStruct((tokens, model), BF16)] * n
    out_specs = [x_spec] * n
    in_specs = [meta_spec(tokens, model)] * len(metas)
    if grads is None:
        kernel, extra = combine_grad_kernel, []
        scratch = [pltpu.VMEM((n, groups * capacity, tokens), BF16)]
    else:
        kernel, extra = combine_out_kernel, grads
        in_specs = in_specs + [x_spec] * len(grads)
        out_shape = out_shape + [jax.ShapeDtypeStruct((n, chosen, tokens), F32)]
        out_specs = out_specs + [whole((n, chosen, tokens))]
        shape = (n, groups * capacity, tokens)
        scratch = [pltpu.VMEM(shape, x) for x in (F32, BF16, BF16, F32)]
    return pl.pallas_call(
        functools.partial(kernel, n, chosen),
        out_shape=out_shape,
        grid_spec=pltpu.PrefetchScalarGridSpec(
            num_scalar_prefetch=1,
            grid=(n,),
            in_specs=in_specs + [back_spec],
            out_specs=out_specs,
            scratch_shapes=scratch,
        ),
        compiler_params=params(),
    )(level, *metas, *extra, back)


def spans(weights):
    start = 0
    for weight in weights:
        yield weight, slice(start, start + weight.shape[0])
        start += weight.shape[0]


def times(rows_ref, weights):
    return sum(dot(rows_ref[:, span], w[...], ((1,), (0,))) for w, span in spans(weights))


def hidden_kernel(count, *refs):
    rows_ref, gates, ups = refs[0], refs[1 : 1 + count], refs[1 + count : 1 + 2 * count]
    hidden_ref, active_ref, slope_ref = refs[1 + 2 * count :]
    gate, up = times(rows_ref, gates), times(rows_ref, ups)
    sigmoid = jax.nn.sigmoid(gate)
    active = gate * sigmoid
    hidden_ref[...] = (active * up).astype(BF16)
    active_ref[...] = active
    slope_ref[...] = up * (sigmoid * (1.0 + gate * (1.0 - sigmoid)))


def hidden_pass(rows, gates, ups, tile):
    slots, model = rows.shape
    units = gates[0].shape[1]
    out_spec = pl.BlockSpec((tile, units), lambda i: (i, 0))
    return pl.pallas_call(
        functools.partial(hidden_kernel, len(gates)),
        out_shape=(
            jax.ShapeDtypeStruct((slots, units), BF16),
            jax.ShapeDtypeStruct((slots, units), F32),
            jax.ShapeDtypeStruct((slots, units), F32),
        ),
        grid=(slots // tile,),
        in_specs=[pl.BlockSpec((tile, model), lambda i: (i, 0))]
        + [whole(w.shape) for w in gates + ups],
        out_specs=(out_spec, out_spec, out_spec),
        compiler_params=params(),
    )(rows, *gates, *ups)


def down_kernel(count, *refs):
    hidden_ref, cotangent_ref, active_ref, slope_ref = refs[:4]
    downs = refs[4 : 4 + count]
    out_ref, gate_ref, up_ref = refs[4 + count :]
    hidden = hidden_ref[...]
    for weight, span in spans(downs):
        out_ref[:, span] = dot(hidden, weight[...], ((1,), (1,))).astype(BF16)
    grad = times(cotangent_ref, downs)
    gate_ref[...] = (grad * slope_ref[...]).astype(BF16)
    up_ref[...] = (grad * active_ref[...]).astype(BF16)


def down_pass(hidden, cotangent, active, slope, downs, tile):
    slots, model = cotangent.shape
    units = hidden.shape[1]
    unit_spec = pl.BlockSpec((tile, units), lambda i: (i, 0))
    model_spec = pl.BlockSpec((tile, model), lambda i: (i, 0))
    return pl.pallas_call(
        functools.partial(down_kernel, len(downs)),
        out_shape=(
            jax.ShapeDtypeStruct((slots, model), BF16),
            jax.ShapeDtypeStruct((slots, units), BF16),
            jax.ShapeDtypeStruct((slots, units), BF16),
        ),
        grid=(slots // tile,),
        in_specs=[unit_spec, model_spec, unit_spec, unit_spec]
        + [whole(w.shape) for w in downs],
        out_specs=(model_spec, unit_spec, unit_spec),
        compiler_params=params(),
    )(hidden, cotangent, active, slope, *downs)


def row_grad_kernel(count, *refs):
    gate_ref, up_ref = refs[:2]
    gates, ups, out_ref = refs[2 : 2 + count], refs[2 + count : 2 + 2 * count], refs[-1]
    for (gate, span), up in zip(spans(gates), ups):
        total = dot(gate_ref[...], gate[...], ((1,), (1,)))
        total += dot(up_ref[...], up[...], ((1,), (1,)))
        out_ref[:, span] = total.astype(BF16)


def row_grad_pass(gate_part, up_part, gates, ups, tile):
    slots, units = gate_part.shape
    model = sum(w.shape[0] for w in gates)
    unit_spec = pl.BlockSpec((tile, units), lambda i: (i, 0))
    return pl.pallas_call(
        functools.partial(row_grad_kernel, len(gates)),
        out_shape=jax.ShapeDtypeStruct((slots, model), BF16),
        grid=(slots // tile,),
        in_specs=[unit_spec, unit_spec] + [whole(w.shape) for w in gates + ups],
        out_specs=pl.BlockSpec((tile, model), lambda i: (i, 0)),
        compiler_params=params(),
    )(gate_part, up_part, *gates, *ups)


def weight_grad_kernel(rows_ref, *refs):
    half = len(refs) // 2
    for part_ref, out_ref in zip(refs[:half], refs[half:]):
        out_ref[...] = dot(rows_ref[...], part_ref[...], ((0,), (0,))).astype(BF16)


def weight_grad(rows, parts, place, width):
    slots, columns = parts[0].shape
    tile = columns // 2 if columns % 256 == 0 else columns
    count = len(parts)
    return pl.pallas_call(
        weight_grad_kernel,
        out_shape=[jax.ShapeDtypeStruct((width, columns), BF16)] * count,
        grid=(columns // tile,),
        in_specs=[pl.BlockSpec((slots, width), lambda i: (0, place))]
        + [pl.BlockSpec((slots, tile), lambda i: (0, i))] * count,
        out_specs=[pl.BlockSpec((width, tile), lambda i: (0, i))] * count,
        compiler_params=params(),
    )(rows, *parts)


def on_device(tokens, out_grad, routes, route_gates, expert_weights):
    groups = lax.axis_size("wide")
    n = lax.axis_size("narrow")
    me = lax.axis_index("narrow")
    experts = groups * n
    token_count, model = tokens.shape
    chosen = routes.shape[1]
    capacity = 2 * chosen * token_count // experts
    slots = experts * capacity
    width = model // n
    units = expert_weights.shape[2] // 3
    level = me.astype(jnp.int32).reshape(1)
    tile = min(256, slots)

    high = lax.reduce_precision(route_gates, 8, 7)
    middle = lax.reduce_precision(route_gates - high, 8, 7)
    low = route_gates - high - middle
    thirds = [x.astype(BF16) for x in (high, middle, low)]
    pad = jnp.zeros((token_count, META - 4 * chosen), BF16)
    sent = jnp.concatenate([tokens, routes.astype(BF16), *thirds, pad], axis=1)
    middle = n // 2
    others = [k for k in range(1, n) if k != middle]
    blocks = split_shard(level, expert_weights, units)
    lanes = Lanes(LANES, ())

    def halves(k):
        return 2 if k == middle else 1

    def swap(x):
        x = x.reshape(groups, n, capacity, model)
        return lax.all_to_all(x, "wide", split_axis=0, concat_axis=0, tiled=True)

    def place(x, gated):
        token_blocks = part("token_blocks")
        return dispatch(
            level, token_blocks, blocks=x, groups=groups, capacity=capacity, chosen=chosen, gated=gated
        )

    def gated(name, x):
        waits = [
            part(y) if isinstance(y, str) else lanes.sent[y * n // 4] for y in GATES.get(name, ())
        ]
        return after(x, *waits) if waits else x

    def hop_on(ups, downs, name):
        step = len(ups)
        up, down = gated(name, (ups[-1], downs[-1]))
        ups.append(hop(up, True, range(step - 1, n - 1)))
        downs.append(hop(down, False, range(1, n - step + 1)))

    def moved(group):
        return [x for k in range(n) for x in came[group][k]]

    came = [{0: [x[0]]} for x in blocks] + [{} for _ in blocks]
    part = Parts()
    steps = [n - 1 if i == 3 else i * (n - 1) // 3 for i in range(4)]
    lines = {"t": ([sent], [sent]), "g": ([out_grad], [out_grad])}

    def line_part(letter, i):
        def make():
            if i > 1:
                part(f"{letter}{i - 1}")
            ups, downs = lines[letter]
            while len(ups) <= steps[i]:
                hop_on(ups, downs, f"{letter}{i}")
            return ups[-1], downs[-1]

        return make

    def sum_part(letter, i):
        def make():
            last = part(f"{letter}{i - 1}") if i > 1 else None
            parts = part("out_parts" if letter == "o" else "grad_parts")
            for step in range(steps[i - 1] + 1, steps[i] + 1):
                last = reduce_step(parts, last, step)
            return last

        return make

    for i in (1, 2, 3):
        for letter in "tg":
            setattr(part, f"{letter}{i}", line_part(letter, i))
        for letter in "or":
            setattr(part, f"{letter}{i}", sum_part(letter, i))

    def define(make):
        setattr(part, make.__name__, make)

    @define
    def split():
        return blocks

    @define
    def token_blocks():
        part("t3")
        return lines["t"][0] + lines["t"][1][1:]

    @define
    def grad_blocks():
        part("g3")
        return lines["g"][0] + lines["g"][1][1:]

    @define
    def rows():
        return swap(place(part("token_blocks"), False)).reshape(slots, model)

    @define
    def cotangent():
        return swap(place(part("grad_blocks"), True)).reshape(slots, model)

    @define
    def units_pass():
        return hidden_pass(gated("units_pass", part("rows")), moved(0), moved(1), tile)

    def grad_pieces(k, rows, *parts):
        made = [
            weight_grad(rows, parts, k * halves(k) + i, width // halves(k))
            for i in range(halves(k))
        ]
        return [[x[j] for x in made] for j in range(len(parts))]

    def down_grad(k, name):
        return grad_pieces(k, part("cotangent"), gated(name, part("units_pass")[0]))[0]

    def in_grad(k, name):
        _, gate_part, up_part = part("down")
        return grad_pieces(k, part("rows"), gated(name, gate_part), up_part)

    @define
    def middle_down_grad():
        return {middle: down_grad(middle, "middle_down_grad")}

    @define
    def other_down_grads():
        return {k: down_grad(k, "other_down_grads") for k in others}

    @define
    def own_down_grad():
        return {0: down_grad(0, "own_down_grad")}

    @define
    def down():
        hidden, active, slope = part("units_pass")
        return down_pass(gated("down", hidden), part("cotangent"), active, slope, moved(2), tile)

    @define
    def middle_in_grad():
        return {middle: in_grad(middle, "middle_in_grad")}

    @define
    def other_in_grads():
        return {k: in_grad(k, "other_in_grads") for k in others}

    @define
    def own_in_grad():
        return {0: in_grad(0, "own_in_grad")}

    @define
    def row_grad():
        _, gate_part, up_part = part("down")
        return row_grad_pass(gated("row_grad", gate_part), up_part, moved(0), moved(1), tile)

    @define
    def back_out():
        return swap(gated("back_out", part("down")[0]))

    @define
    def back_grad():
        return swap(gated("back_grad", after(part("row_grad"), part("back_out"))))

    @define
    def out_sums():
        back = gated("out_sums", part("back_out"))
        return combine(level, part("token_blocks"), back, chosen, part("grad_blocks"))

    @define
    def out_parts():
        return part("out_sums")[:-1]

    @define
    def grad_parts():
        return combine(level, part("token_blocks"), gated("grad_parts", part("back_grad")), chosen)

    @define
    def gate_grad():
        dots = gated("gate_grad", part("out_sums")[-1])
        return dots[0] + sum(shift(dots[d], -d) for d in range(1, n))

    def joined(group, name, shard=None):
        grads = [part(own)[0] for own in ("own_down_grad",)] if group == 2 else None
        if grads is None:
            grads = [part("own_in_grad")[0][group]]
        grads = [jnp.concatenate(x) for x in grads]
        grads += [jnp.concatenate(came[3 + group][k]) for k in range(1, n)]
        return join_shard(level, gated(name, grads), 3 * units, group, shard)

    def pieces_of(group, back, k):
        if not back:
            return jnp.split(blocks[group][k], halves(k))
        name = "middle" if k == middle else "other"
        if group == 2:
            return part("middle_down_grad" if k == middle else "other_down_grads")[k]
        return part("middle_in_grad" if k == middle else "other_in_grads")[k][group]

    part("t1")
    lanes.latest = [part("t1")] * LANES
    for back, turns in ((False, (0, 1, 2)), (True, BACK_TURNS)):
        for group in turns:
            order = [middle, *others] if MIDDLE_FIRST[back] else [*others, middle]
            for k in order:
                arrived = came[group + (3 if back else 0)].setdefault(k, [])
                for i in range(halves(k)):
                    names = WAITS.get(len(lanes.sent) * 4 // n, ())
                    names = names if len(lanes.sent) % max(1, n // 4) == 0 else ()
                    waits = [part(name) for name in names]
                    x = pieces_of(group, back, k)[i]
                    arrived.append(lanes.send(x, -k if back else k, waits))
    layer_output = reduce_end(part("out_parts"), part("o3"))
    token_grad = reduce_end(part("grad_parts"), part("r3"))
    shard = None
    for i, group in enumerate(BACK_TURNS):
        shard = joined(group, f"join{i}", shard)
    return (layer_output, token_grad, part("gate_grad").T, shard)


def solution(mesh):
    return jax.shard_map(
        on_device,
        mesh=mesh,
        in_specs=(
            P(("wide", "narrow"), None),
            P(("wide", "narrow"), None),
            P(("wide", "narrow"), None),
            P(("wide", "narrow"), None),
            P("narrow", "wide", None),
        ),
        out_specs=(
            P(("wide", "narrow"), None),
            P(("wide", "narrow"), None),
            P(("wide", "narrow"), None),
            P("narrow", "wide", None),
        ),
        check_vma=False,
    )
```

```python
import functools

import jax
import jax.numpy as jnp
from jax import lax
from jax.experimental import pallas as pl
from jax.experimental.pallas import tpu as pltpu
from jax.sharding import PartitionSpec as P

F32 = jnp.float32
BF16 = jnp.bfloat16
VMEM_LIMIT = 50 * 1024 * 1024
META = 128
LANES = 2
FLOPS_PER_VALUE = 40000
BACK_TURNS = (2, 0, 1)
MIDDLE_FIRST = (False, False)
WAITS = {3: ['t2'],
 4: ['g1'],
 5: ['t3'],
 6: ['g2'],
 7: ['g3'],
 10: ['units_pass', 'cotangent'],
 12: ['middle_down_grad', 'own_down_grad', 'other_down_grads'],
 17: ['row_grad'],
 18: ['back_out'],
 19: ['out_parts'],
 20: ['o1'],
 21: ['o2'],
 22: ['o3', 'grad_parts', 'gate_grad', 'back_grad']}
GATES = {'back_out': [12],
 'down': ['other_down_grads', 'middle_down_grad', 'own_down_grad'],
 'g1': ['t1'],
 'grad_parts': [19],
 'join0': [19],
 'join1': [21],
 'middle_in_grad': [16],
 'other_in_grads': [13],
 'out_sums': [16],
 'own_in_grad': [18],
 'row_grad': ['other_in_grads', 14],
 't2': ['split']}


def dot(a, b, dims):
    return lax.dot_general(a, b, (dims, ((), ())), preferred_element_type=F32)


def params():
    return pltpu.CompilerParams(vmem_limit_bytes=VMEM_LIMIT)


def whole(shape):
    return pl.BlockSpec(shape, lambda *_: (0,) * len(shape))


def after(x, *others):
    return lax.optimization_barrier((x, others))[0]


def shift(x, k):
    n = lax.axis_size("narrow")
    return lax.ppermute(x, "narrow", [(i, (i + k) % n) for i in range(n)])


def arrival_kernel(moved_ref, out_ref, done_ref):
    done_ref[...] = jnp.zeros_like(done_ref)


def arrival(moved, load):
    anywhere = pl.BlockSpec(memory_space=pl.ANY)
    return pl.pallas_call(
        arrival_kernel,
        out_shape=jax.ShapeDtypeStruct(moved.shape, moved.dtype),
        in_specs=[anywhere],
        out_specs=anywhere,
        scratch_shapes=[pltpu.VMEM((8, 128), F32)],
        input_output_aliases={0: 0},
        cost_estimate=pl.CostEstimate(
            flops=FLOPS_PER_VALUE * moved.size * load, bytes_accessed=0, transcendentals=0
        ),
    )(moved)


class Lanes:
    def __init__(self, count, first):
        self.latest = [first] * count
        self.sent = []

    def send(self, x, k, others=()):
        lane = len(self.sent) % len(self.latest)
        n = lax.axis_size("narrow")
        moved = shift(after(x, self.latest[lane], others), k)
        moved = arrival(moved, min(k % n, -k % n))
        self.latest[lane] = moved
        self.sent.append(moved)
        return moved


class Parts:
    def __init__(self):
        self.made = {}

    def __call__(self, name):
        if name not in self.made:
            self.made[name] = getattr(self, name)()
        return self.made[name]


def hop(x, up, sources):
    step = 1 if up else -1
    return lax.ppermute(x, "narrow", [(i, i + step) for i in sources])


def reduce_step(parts, last, step):
    n = len(parts)
    up_send, down_send = parts[step], parts[n - step]
    if last is not None:
        up_send = (up_send.astype(F32) + last[0].astype(F32)).astype(BF16)
        down_send = (down_send.astype(F32) + last[1].astype(F32)).astype(BF16)
    return hop(up_send, True, range(step)), hop(down_send, False, range(n - step, n))


def reduce_end(parts, last):
    total = parts[0].astype(F32) + last[0].astype(F32) + last[1].astype(F32)
    return total.astype(BF16)


def mixing(level, n, depth):
    row = lax.broadcasted_iota(jnp.int32, (n * depth, n * depth), 0)
    column = lax.broadcasted_iota(jnp.int32, (n * depth, n * depth), 1)
    same = (row // n == column % depth) & (row % n == lax.rem(level + column // depth, n))
    return jnp.where(same, 1.0, 0.0).astype(BF16)


def split_kernel(n, level_ref, shard_ref, *out_refs):
    depth, _, columns = shard_ref.shape
    part = out_refs[0].shape[1]
    shard = shard_ref[...].reshape(depth * n, columns)
    apart = dot(mixing(level_ref[0], n, depth), shard, ((0,), (0,))).astype(BF16)
    for i, out_ref in enumerate(out_refs):
        k, group = i % n, i // n
        out_ref[...] = apart[k * depth : (k + 1) * depth, group * part : (group + 1) * part]


def split_shard(level, shard, part):
    rows, n, columns = shard.shape
    depth = min(rows, 256 // n)
    count = columns // part
    outs = pl.pallas_call(
        functools.partial(split_kernel, n),
        out_shape=[jax.ShapeDtypeStruct((rows, part), BF16)] * (n * count),
        grid_spec=pltpu.PrefetchScalarGridSpec(
            num_scalar_prefetch=1,
            grid=(rows // depth,),
            in_specs=[pl.BlockSpec((depth, n, columns), lambda i, level: (i, 0, 0))],
            out_specs=[pl.BlockSpec((depth, part), lambda i, level: (i, 0))] * (n * count),
        ),
        compiler_params=params(),
    )(level, shard)
    return [outs[i * n : (i + 1) * n] for i in range(count)]


def join_kernel(n, level_ref, *refs):
    out_ref = refs[-1]
    depth, _, columns = out_ref.shape
    apart = jnp.concatenate([ref[...] for ref in refs[:n]], axis=0)
    mixed = dot(mixing(level_ref[0], n, depth), apart, ((1,), (0,)))
    out_ref[...] = mixed.astype(BF16).reshape(depth, n, columns)


def join_shard(level, blocks, columns, place, shard=None):
    n = len(blocks)
    rows, part = blocks[0].shape
    depth = min(rows, 256 // n)
    more = [] if shard is None else [shard]
    return pl.pallas_call(
        functools.partial(join_kernel, n),
        out_shape=jax.ShapeDtypeStruct((rows, n, columns), BF16),
        grid_spec=pltpu.PrefetchScalarGridSpec(
            num_scalar_prefetch=1,
            grid=(rows // depth,),
            in_specs=[pl.BlockSpec((depth, part), lambda i, level: (i, 0))] * n
            + [pl.BlockSpec(memory_space=pl.ANY)] * len(more),
            out_specs=pl.BlockSpec((depth, n, part), lambda i, level: (i, 0, place)),
        ),
        input_output_aliases={1 + n: 0} if more else {},
        compiler_params=params(),
    )(level, *blocks, *more)


def arrived(refs, n, d):
    return refs[0][...] if d == 0 else refs[d][...] + refs[n - 1 + n - d][...]


def slots_of(level, n, groups, chosen, capacity, meta):
    tokens = meta.shape[0]
    lines = jnp.transpose(meta.astype(F32))
    expert = lax.broadcasted_iota(jnp.int32, (groups, tokens), 0) * n + level
    expert = expert.astype(F32)
    named = [lines[k : k + 1] == expert for k in range(chosen)]
    gates = [
        lines[chosen + k : chosen + k + 1]
        + lines[2 * chosen + k : 2 * chosen + k + 1]
        + lines[3 * chosen + k : 3 * chosen + k + 1]
        for k in range(chosen)
    ]
    one = sum(jnp.where(x, 1.0, 0.0) for x in named)
    row = lax.broadcasted_iota(jnp.int32, (tokens, tokens), 0)
    column = lax.broadcasted_iota(jnp.int32, (tokens, tokens), 1)
    earlier = jnp.where(row < column, 1.0, 0.0).astype(BF16)
    rank = dot(one.astype(BF16), earlier, ((1,), (0,)))
    rank = jnp.where(one > 0.5, rank, -1.0).astype(jnp.int32)
    slot = lax.broadcasted_iota(jnp.int32, (groups, capacity, tokens), 1)
    return named, gates, rank[:, None, :] == slot


def gates_of(named, gates):
    return sum(jnp.where(name, gate, 0.0) for name, gate in zip(named, gates))


def dispatch_kernel(n, chosen, gated, level_ref, *refs):
    count = 2 * n - 1
    metas, blocks, out_ref = refs[:count], refs[count : 2 * count], refs[2 * count]
    matrix_ref, weight_ref = refs[2 * count + 1 :]
    groups, _, capacity, width = out_ref.shape

    @pl.when(pl.program_id(0) == 0)
    def _():
        for d in range(n):
            meta = arrived(metas, n, d)
            tokens = meta.shape[0]
            named, gates, taken = slots_of(level_ref[0], n, groups, chosen, capacity, meta)
            matrix = jnp.where(taken, 1.0, 0.0).astype(BF16)
            matrix_ref[d] = matrix.reshape(groups * capacity, tokens)
            if gated:
                weight = jnp.where(taken, gates_of(named, gates)[:, None, :], 0.0)
                weight = jnp.sum(weight, axis=2, keepdims=True)
                weight_ref[d] = weight.reshape(groups * capacity, 1)

    for d in range(n):
        rows = dot(matrix_ref[d], arrived(blocks, n, d), ((1,), (0,)))
        if gated:
            rows = rows * weight_ref[d]
        out_ref[:, d] = rows.astype(BF16).reshape(groups, capacity, width)


def rolled(n, tokens, width):
    return pl.BlockSpec((tokens, width), lambda k, level: (0, lax.rem(level[0] - k + n, n)))


def meta_spec(tokens, model):
    return pl.BlockSpec((tokens, META), lambda k, level: (0, model // META))


def dispatch(level, metas, *, blocks, groups, capacity, chosen, gated):
    n = (len(blocks) + 1) // 2
    tokens, model = blocks[0].shape[0], metas[0].shape[1] - META
    width = model // n
    return pl.pallas_call(
        functools.partial(dispatch_kernel, n, chosen, gated),
        out_shape=jax.ShapeDtypeStruct((groups, n, capacity, model), BF16),
        grid_spec=pltpu.PrefetchScalarGridSpec(
            num_scalar_prefetch=1,
            grid=(n,),
            in_specs=[meta_spec(tokens, model)] * len(metas)
            + [rolled(n, tokens, width)] * len(blocks),
            out_specs=pl.BlockSpec((groups, n, capacity, width), lambda k, level: (0, 0, 0, k)),
            scratch_shapes=[
                pltpu.VMEM((n, groups * capacity, tokens), BF16),
                pltpu.VMEM((n, groups * capacity, 1), F32),
            ],
        ),
        compiler_params=params(),
    )(level, *metas, *blocks)


def combine_out_kernel(n, chosen, level_ref, *refs):
    count = 2 * n - 1
    metas, grads, back_ref = refs[:count], refs[count : 2 * count], refs[2 * count]
    out_refs, dots_ref = refs[2 * count + 1 : 2 * count + 1 + n], refs[2 * count + 1 + n]
    matrix_ref, high_ref, low_ref, pairs_ref = refs[2 * count + 2 + n :]
    groups, _, capacity, width = back_ref.shape
    tokens = metas[0].shape[0]
    step = pl.program_id(0)

    def slots(d):
        return slots_of(level_ref[0], n, groups, chosen, capacity, arrived(metas, n, d))

    @pl.when(step == 0)
    def _():
        for d in range(n):
            named, gates, taken = slots(d)
            weight = jnp.where(taken, gates_of(named, gates)[:, None, :], 0.0)
            weight = weight.reshape(groups * capacity, tokens)
            high = weight.astype(BF16)
            high_ref[d] = high
            low_ref[d] = (weight - high.astype(F32)).astype(BF16)
            matrix = jnp.where(taken, 1.0, 0.0)
            matrix_ref[d] = matrix.reshape(groups * capacity, tokens)
        pairs_ref[...] = jnp.zeros_like(pairs_ref)

    for d in range(n):
        rows = back_ref[:, d].reshape(groups * capacity, width)
        total = dot(high_ref[d], rows, ((0,), (0,))) + dot(low_ref[d], rows, ((0,), (0,)))
        out_refs[d][...] = total.astype(BF16)
        pairs_ref[d] += dot(rows, arrived(grads, n, d), ((1,), (1,)))

    @pl.when(step == n - 1)
    def _():
        for d in range(n):
            named, _, _ = slots(d)
            pairs = pairs_ref[d] * matrix_ref[d]
            pairs = jnp.sum(pairs.reshape(groups, capacity, tokens), axis=1)
            dots_ref[d] = jnp.concatenate(
                [jnp.sum(jnp.where(name, pairs, 0.0), axis=0, keepdims=True) for name in named]
            )


def combine_grad_kernel(n, chosen, level_ref, *refs):
    count = 2 * n - 1
    metas, back_ref, out_refs = refs[:count], refs[count], refs[count + 1 : count + 1 + n]
    matrix_ref = refs[count + 1 + n]
    groups, _, capacity, width = back_ref.shape
    tokens = metas[0].shape[0]

    @pl.when(pl.program_id(0) == 0)
    def _():
        for d in range(n):
            meta = arrived(metas, n, d)
            _, _, taken = slots_of(level_ref[0], n, groups, chosen, capacity, meta)
            matrix = jnp.where(taken, 1.0, 0.0).astype(BF16)
            matrix_ref[d] = matrix.reshape(groups * capacity, tokens)

    for d in range(n):
        rows = back_ref[:, d].reshape(groups * capacity, width)
        out_refs[d][...] = dot(matrix_ref[d], rows, ((0,), (0,))).astype(BF16)


def combine(level, metas, back, chosen, grads=None):
    groups, n, capacity, model = back.shape
    tokens = metas[0].shape[0]
    width = model // n
    x_spec = rolled(n, tokens, width)
    back_spec = pl.BlockSpec((groups, n, capacity, width), lambda k, level: (0, 0, 0, k))
    out_shape = [jax.ShapeDtypeStruct((tokens, model), BF16)] * n
    out_specs = [x_spec] * n
    in_specs = [meta_spec(tokens, model)] * len(metas)
    if grads is None:
        kernel, extra = combine_grad_kernel, []
        scratch = [pltpu.VMEM((n, groups * capacity, tokens), BF16)]
    else:
        kernel, extra = combine_out_kernel, grads
        in_specs = in_specs + [x_spec] * len(grads)
        out_shape = out_shape + [jax.ShapeDtypeStruct((n, chosen, tokens), F32)]
        out_specs = out_specs + [whole((n, chosen, tokens))]
        shape = (n, groups * capacity, tokens)
        scratch = [pltpu.VMEM(shape, x) for x in (F32, BF16, BF16, F32)]
    return pl.pallas_call(
        functools.partial(kernel, n, chosen),
        out_shape=out_shape,
        grid_spec=pltpu.PrefetchScalarGridSpec(
            num_scalar_prefetch=1,
            grid=(n,),
            in_specs=in_specs + [back_spec],
            out_specs=out_specs,
            scratch_shapes=scratch,
        ),
        compiler_params=params(),
    )(level, *metas, *extra, back)


def spans(weights):
    start = 0
    for weight in weights:
        yield weight, slice(start, start + weight.shape[0])
        start += weight.shape[0]


def times(rows_ref, weights):
    return sum(dot(rows_ref[:, span], w[...], ((1,), (0,))) for w, span in spans(weights))


def hidden_kernel(count, *refs):
    rows_ref, gates, ups = refs[0], refs[1 : 1 + count], refs[1 + count : 1 + 2 * count]
    hidden_ref, active_ref, slope_ref = refs[1 + 2 * count :]
    gate, up = times(rows_ref, gates), times(rows_ref, ups)
    sigmoid = jax.nn.sigmoid(gate)
    active = gate * sigmoid
    hidden_ref[...] = (active * up).astype(BF16)
    active_ref[...] = active
    slope_ref[...] = up * (sigmoid * (1.0 + gate * (1.0 - sigmoid)))


def hidden_pass(rows, gates, ups, tile):
    slots, model = rows.shape
    units = gates[0].shape[1]
    out_spec = pl.BlockSpec((tile, units), lambda i: (i, 0))
    return pl.pallas_call(
        functools.partial(hidden_kernel, len(gates)),
        out_shape=(
            jax.ShapeDtypeStruct((slots, units), BF16),
            jax.ShapeDtypeStruct((slots, units), F32),
            jax.ShapeDtypeStruct((slots, units), F32),
        ),
        grid=(slots // tile,),
        in_specs=[pl.BlockSpec((tile, model), lambda i: (i, 0))]
        + [whole(w.shape) for w in gates + ups],
        out_specs=(out_spec, out_spec, out_spec),
        compiler_params=params(),
    )(rows, *gates, *ups)


def down_kernel(count, *refs):
    hidden_ref, cotangent_ref, active_ref, slope_ref = refs[:4]
    downs = refs[4 : 4 + count]
    out_ref, gate_ref, up_ref = refs[4 + count :]
    hidden = hidden_ref[...]
    for weight, span in spans(downs):
        out_ref[:, span] = dot(hidden, weight[...], ((1,), (1,))).astype(BF16)
    grad = times(cotangent_ref, downs)
    gate_ref[...] = (grad * slope_ref[...]).astype(BF16)
    up_ref[...] = (grad * active_ref[...]).astype(BF16)


def down_pass(hidden, cotangent, active, slope, downs, tile):
    slots, model = cotangent.shape
    units = hidden.shape[1]
    unit_spec = pl.BlockSpec((tile, units), lambda i: (i, 0))
    model_spec = pl.BlockSpec((tile, model), lambda i: (i, 0))
    return pl.pallas_call(
        functools.partial(down_kernel, len(downs)),
        out_shape=(
            jax.ShapeDtypeStruct((slots, model), BF16),
            jax.ShapeDtypeStruct((slots, units), BF16),
            jax.ShapeDtypeStruct((slots, units), BF16),
        ),
        grid=(slots // tile,),
        in_specs=[unit_spec, model_spec, unit_spec, unit_spec]
        + [whole(w.shape) for w in downs],
        out_specs=(model_spec, unit_spec, unit_spec),
        compiler_params=params(),
    )(hidden, cotangent, active, slope, *downs)


def row_grad_kernel(count, *refs):
    gate_ref, up_ref = refs[:2]
    gates, ups, out_ref = refs[2 : 2 + count], refs[2 + count : 2 + 2 * count], refs[-1]
    for (gate, span), up in zip(spans(gates), ups):
        total = dot(gate_ref[...], gate[...], ((1,), (1,)))
        total += dot(up_ref[...], up[...], ((1,), (1,)))
        out_ref[:, span] = total.astype(BF16)


def row_grad_pass(gate_part, up_part, gates, ups, tile):
    slots, units = gate_part.shape
    model = sum(w.shape[0] for w in gates)
    unit_spec = pl.BlockSpec((tile, units), lambda i: (i, 0))
    return pl.pallas_call(
        functools.partial(row_grad_kernel, len(gates)),
        out_shape=jax.ShapeDtypeStruct((slots, model), BF16),
        grid=(slots // tile,),
        in_specs=[unit_spec, unit_spec] + [whole(w.shape) for w in gates + ups],
        out_specs=pl.BlockSpec((tile, model), lambda i: (i, 0)),
        compiler_params=params(),
    )(gate_part, up_part, *gates, *ups)


def weight_grad_kernel(rows_ref, *refs):
    half = len(refs) // 2
    for part_ref, out_ref in zip(refs[:half], refs[half:]):
        out_ref[...] = dot(rows_ref[...], part_ref[...], ((0,), (0,))).astype(BF16)


def weight_grad(rows, parts, place, width):
    slots, columns = parts[0].shape
    tile = columns // 2 if columns % 256 == 0 else columns
    count = len(parts)
    return pl.pallas_call(
        weight_grad_kernel,
        out_shape=[jax.ShapeDtypeStruct((width, columns), BF16)] * count,
        grid=(columns // tile,),
        in_specs=[pl.BlockSpec((slots, width), lambda i: (0, place))]
        + [pl.BlockSpec((slots, tile), lambda i: (0, i))] * count,
        out_specs=[pl.BlockSpec((width, tile), lambda i: (0, i))] * count,
        compiler_params=params(),
    )(rows, *parts)


def on_device(tokens, out_grad, routes, route_gates, expert_weights):
    groups = lax.axis_size("wide")
    n = lax.axis_size("narrow")
    me = lax.axis_index("narrow")
    experts = groups * n
    token_count, model = tokens.shape
    chosen = routes.shape[1]
    capacity = 2 * chosen * token_count // experts
    slots = experts * capacity
    width = model // n
    units = expert_weights.shape[2] // 3
    level = me.astype(jnp.int32).reshape(1)
    tile = min(256, slots)

    high = lax.reduce_precision(route_gates, 8, 7)
    middle = lax.reduce_precision(route_gates - high, 8, 7)
    low = route_gates - high - middle
    thirds = [x.astype(BF16) for x in (high, middle, low)]
    pad = jnp.zeros((token_count, META - 4 * chosen), BF16)
    sent = jnp.concatenate([tokens, routes.astype(BF16), *thirds, pad], axis=1)
    middle = n // 2
    others = [k for k in range(1, n) if k != middle]
    blocks = split_shard(level, expert_weights, units)
    lanes = Lanes(LANES, ())

    def halves(k):
        return 2 if k == middle else 1

    def swap(x):
        x = x.reshape(groups, n, capacity, model)
        return lax.all_to_all(x, "wide", split_axis=0, concat_axis=0, tiled=True)

    def place(x, gated):
        token_blocks = part("token_blocks")
        return dispatch(
            level, token_blocks, blocks=x, groups=groups, capacity=capacity, chosen=chosen, gated=gated
        )

    def gated(name, x):
        waits = [
            part(y) if isinstance(y, str) else lanes.sent[y * n // 4] for y in GATES.get(name, ())
        ]
        return after(x, *waits) if waits else x

    def hop_on(ups, downs, name):
        step = len(ups)
        up, down = gated(name, (ups[-1], downs[-1]))
        ups.append(hop(up, True, range(step - 1, n - 1)))
        downs.append(hop(down, False, range(1, n - step + 1)))

    def moved(group):
        return [x for k in range(n) for x in came[group][k]]

    came = [{0: [x[0]]} for x in blocks] + [{} for _ in blocks]
    part = Parts()
    steps = [n - 1 if i == 3 else i * (n - 1) // 3 for i in range(4)]
    lines = {"t": ([sent], [sent]), "g": ([out_grad], [out_grad])}

    def line_part(letter, i):
        def make():
            if i > 1:
                part(f"{letter}{i - 1}")
            ups, downs = lines[letter]
            while len(ups) <= steps[i]:
                hop_on(ups, downs, f"{letter}{i}")
            return ups[-1], downs[-1]

        return make

    def sum_part(letter, i):
        def make():
            last = part(f"{letter}{i - 1}") if i > 1 else None
            parts = part("out_parts" if letter == "o" else "grad_parts")
            for step in range(steps[i - 1] + 1, steps[i] + 1):
                last = reduce_step(parts, last, step)
            return last

        return make

    for i in (1, 2, 3):
        for letter in "tg":
            setattr(part, f"{letter}{i}", line_part(letter, i))
        for letter in "or":
            setattr(part, f"{letter}{i}", sum_part(letter, i))

    def define(make):
        setattr(part, make.__name__, make)

    @define
    def split():
        return blocks

    @define
    def token_blocks():
        part("t3")
        return lines["t"][0] + lines["t"][1][1:]

    @define
    def grad_blocks():
        part("g3")
        return lines["g"][0] + lines["g"][1][1:]

    @define
    def rows():
        return swap(place(part("token_blocks"), False)).reshape(slots, model)

    @define
    def cotangent():
        return swap(place(part("grad_blocks"), True)).reshape(slots, model)

    @define
    def units_pass():
        return hidden_pass(gated("units_pass", part("rows")), moved(0), moved(1), tile)

    def grad_pieces(k, rows, *parts):
        made = [
            weight_grad(rows, parts, k * halves(k) + i, width // halves(k))
            for i in range(halves(k))
        ]
        return [[x[j] for x in made] for j in range(len(parts))]

    def down_grad(k, name):
        return grad_pieces(k, part("cotangent"), gated(name, part("units_pass")[0]))[0]

    def in_grad(k, name):
        _, gate_part, up_part = part("down")
        return grad_pieces(k, part("rows"), gated(name, gate_part), up_part)

    @define
    def middle_down_grad():
        return {middle: down_grad(middle, "middle_down_grad")}

    @define
    def other_down_grads():
        return {k: down_grad(k, "other_down_grads") for k in others}

    @define
    def own_down_grad():
        return {0: down_grad(0, "own_down_grad")}

    @define
    def down():
        hidden, active, slope = part("units_pass")
        return down_pass(gated("down", hidden), part("cotangent"), active, slope, moved(2), tile)

    @define
    def middle_in_grad():
        return {middle: in_grad(middle, "middle_in_grad")}

    @define
    def other_in_grads():
        return {k: in_grad(k, "other_in_grads") for k in others}

    @define
    def own_in_grad():
        return {0: in_grad(0, "own_in_grad")}

    @define
    def row_grad():
        _, gate_part, up_part = part("down")
        return row_grad_pass(gated("row_grad", gate_part), up_part, moved(0), moved(1), tile)

    @define
    def back_out():
        return swap(gated("back_out", part("down")[0]))

    @define
    def back_grad():
        return swap(gated("back_grad", after(part("row_grad"), part("back_out"))))

    @define
    def out_sums():
        back = gated("out_sums", part("back_out"))
        return combine(level, part("token_blocks"), back, chosen, part("grad_blocks"))

    @define
    def out_parts():
        return part("out_sums")[:-1]

    @define
    def grad_parts():
        return combine(level, part("token_blocks"), gated("grad_parts", part("back_grad")), chosen)

    @define
    def gate_grad():
        dots = gated("gate_grad", part("out_sums")[-1])
        return dots[0] + sum(shift(dots[d], -d) for d in range(1, n))

    def joined(group, name, shard=None):
        grads = [part(own)[0] for own in ("own_down_grad",)] if group == 2 else None
        if grads is None:
            grads = [part("own_in_grad")[0][group]]
        grads = [jnp.concatenate(x) for x in grads]
        grads += [jnp.concatenate(came[3 + group][k]) for k in range(1, n)]
        return join_shard(level, gated(name, grads), 3 * units, group, shard)

    def pieces_of(group, back, k):
        if not back:
            return jnp.split(blocks[group][k], halves(k))
        name = "middle" if k == middle else "other"
        if group == 2:
            return part("middle_down_grad" if k == middle else "other_down_grads")[k]
        return part("middle_in_grad" if k == middle else "other_in_grads")[k][group]

    part("t1")
    lanes.latest = [part("t1")] * LANES
    for back, turns in ((False, (0, 1, 2)), (True, BACK_TURNS)):
        for group in turns:
            order = [middle, *others] if MIDDLE_FIRST[back] else [*others, middle]
            for k in order:
                arrived = came[group + (3 if back else 0)].setdefault(k, [])
                for i in range(halves(k)):
                    names = WAITS.get(len(lanes.sent) * 4 // n, ())
                    names = names if len(lanes.sent) % max(1, n // 4) == 0 else ()
                    waits = [part(name) for name in names]
                    x = pieces_of(group, back, k)[i]
                    arrived.append(lanes.send(x, -k if back else k, waits))
    layer_output = reduce_end(part("out_parts"), part("o3"))
    token_grad = reduce_end(part("grad_parts"), part("r3"))
    shard = None
    for i, group in enumerate(BACK_TURNS):
        shard = joined(group, f"join{i}", shard)
    return (layer_output, token_grad, part("gate_grad").T, shard)


def solution(mesh):
    return jax.shard_map(
        on_device,
        mesh=mesh,
        in_specs=(
            P(("wide", "narrow"), None),
            P(("wide", "narrow"), None),
            P(("wide", "narrow"), None),
            P(("wide", "narrow"), None),
            P("narrow", "wide", None),
        ),
        out_specs=(
            P(("wide", "narrow"), None),
            P(("wide", "narrow"), None),
            P(("wide", "narrow"), None),
            P("narrow", "wide", None),
        ),
        check_vma=False,
    )
```
